32 devices in a mesh: dp: 2 (over y), expert: 16 (over z, x, core).
Axes of the slice: x: 2, y: 2, z: 4, core: 2. Of those that a mesh axis runs over, the one named last changes fastest.
Arguments:
- tokens: bfloat16 [2048, 4096], P('expert', 'dp'), may hold values from -6 to 6
- cotangent: bfloat16 [2048, 4096], P('expert', 'dp'), may hold values from -1.5 to 1.5
- router_probs: bfloat16 [2048, 8], P('expert'), may hold values from 0.049804688 to 1
- expert_ids: int32 [2048, 8], P('expert'), may hold values from 0 to 15, all different within a row; in each aligned block of 128 rows (0 to 127, 128 to 255, ...) at most 68 rows name the same one
- w_gate: bfloat16 [16, 768, 4096], P('expert', None, 'dp'), may hold values from -0.09375 to 0.09375
- w_up: bfloat16 [16, 768, 4096], P('expert', None, 'dp'), may hold values from -0.09375 to 0.09375
- w_down: bfloat16 [16, 768, 4096], P('expert', None, 'dp'), may hold values from -0.21875 to 0.21875
Outputs:
- token_grads: bfloat16 [2048, 4096], P('expert', 'dp')
- prob_grads: float32 [2048, 8], P('expert')
- gate_grads: bfloat16 [16, 768, 4096], P('expert', None, 'dp')
- up_grads: bfloat16 [16, 768, 4096], P('expert', None, 'dp')
- down_grads: bfloat16 [16, 768, 4096], P('expert', None, 'dp')
The draws below stay inside these ranges and needn't reach their ends.
Inputs may be any that keep to these rules, and one draw needn't show every extreme that they name: `expert_ids`: each row names 8 different experts. Among the 128 tokens of one index of expert no expert is named more than 68 times, a bound that some block reaches.
All inputs are finite; a program needn't handle non-finite values.
Results may differ from the reference program's by a relative error of at most 0.02.
Values may be sent and summed in bfloat16 or wider, within the bound.
No kernel may reach another device: no remote copies, remote signals or barrier semaphores. Data moves between devices by JAX's collectives and lax.ppermute only.
A program may use at most 128 MiB of HBM per device.

```python
import math
import jax
import jax.numpy as jnp
import numpy as np
from jax import lax

D = 4096
FF = 768
TOPK = 8
TOK_DEV = 128
EXPERTS = 16
TOKENS = 2048
SLOTS = 68
N_DP = 2
N_EXPERT = 16


def block_scale(rng, extent, shards, low, largest):
    loudness, own = 1.0, jax.random.fold_in(rng, 6)
    for dim, blocks in shards:
        heights = jnp.exp(jax.random.uniform(jax.random.fold_in(own, dim), (blocks,), jnp.float32, low / len(shards), largest / len(shards)))
        loudness = loudness * jnp.repeat(heights, extent[dim] // blocks).reshape([-1 if axis == dim else 1 for axis in range(len(extent))])
    return loudness


def assign_block(rng, own, number, rows, count, top, reach, slope):
    ranking = jax.random.permutation(rng, count)
    heavy_load, ordinary = shares(count, rows * top, reach, slope, True), shares(count, rows * top, reach, slope, False)
    places = jnp.arange(count)

    def named(lengths, rotation):
        used = int((lengths > 0).sum())
        fixed = max(1, used // 4)
        shifted = fixed + (places - fixed + rotation * (used - fixed)) % max(1, count - fixed)
        return jnp.zeros((count,), jnp.int32).at[ranking[jnp.where(places < fixed, places, shifted)]].set(jnp.asarray(lengths, jnp.int32))

    lengths = jnp.where(number % 4 == 0, named(heavy_load, number // 4), named(ordinary, number - number // 4 - 1))
    mixed = jax.random.permutation(jax.random.fold_in(own, 3), count)
    donor, taker = mixed[0:count // 2 * 2:2], mixed[1:count // 2 * 2:2]
    slack = jnp.minimum(lengths[donor] - 1, reach - lengths[taker]) // 2
    slack = jnp.where((donor == ranking[0]) | (taker == ranking[0]) | (lengths[taker] == 0), 0, jnp.maximum(slack, 0))
    shifted = jax.random.randint(jax.random.fold_in(own, 4), (count // 2,), 0, 1 << 20) % (slack + 1)
    lengths = lengths.at[donor].add(-shifted).at[taker].add(shifted)
    items = jnp.searchsorted(jnp.cumsum(lengths), jnp.arange(rows * top), side="right").astype(jnp.int32)
    grid = items.reshape(top, rows).T
    grid = grid[jax.random.permutation(jax.random.fold_in(own, 1), rows)]
    rotation = jax.random.randint(jax.random.fold_in(own, 2), (rows, 1), 0, top)
    return jnp.take_along_axis(grid, (jnp.arange(top)[None, :] + rotation) % top, axis=1)


def shares(count, total, limit, slope, full):
    portions = [(1 << 20) // math.isqrt(rank ** slope) + 1 for rank in range(1, count + 1)]
    largest = limit if full else min(limit, max(-(-total // count), total * portions[0] // sum(portions)))
    least = 1 if total - largest >= count - 1 else 0
    given, rest = [largest] + [least] * (count - 1), total - largest - least * (count - 1)
    while rest > 0:
        free = [i for i in range(1, count) if given[i] < largest] or [i for i in range(1, count) if given[i] < limit]
        pool, budget = sum([portions[i] for i in free]), rest
        for i in free:
            more = min(limit - given[i], max(1, budget * portions[i] // pool), rest)
            given[i] = given[i] + more
            rest = rest - more
    return np.array(given)


def scatter_about(key, shape, deviation, reach, cuts=(), held_as=jnp.bfloat16):
    factor_of = block_scale(key, shape, cuts, -0.22, 0.18) if cuts else 1.0
    drawn = jax.random.normal(key, shape, jnp.float32) * deviation * factor_of
    return jnp.minimum(jnp.maximum(drawn, -reach), reach).astype(held_as)


def setup_inputs(seed: int = 0) -> dict:
    key_of = jax.random.split(jax.random.key(seed), 8)
    tokens = scatter_about(key_of[0], (TOKENS, D), 1.0, 6.0, ((0, 16), (1, 2)))
    cotangent = scatter_about(key_of[1], (TOKENS, D), 0.25, 1.5, ((0, 16), (1, 2)))
    router_probs = jnp.clip(jnp.exp(math.log(1.0) - 2.9996462 * jax.random.uniform(key_of[2], (TOKENS, TOPK), jnp.float32) ** block_scale(key_of[2], (TOKENS, TOPK), ((0, 16),), -0.2, 0.2)), 0.049804688, 1.0).astype(jnp.bfloat16)
    expert_ids_keys = jax.random.split(jax.random.fold_in(key_of[3], 1), TOKENS // TOK_DEV)
    expert_ids_turns = jax.random.permutation(jax.random.fold_in(key_of[3], 3), TOKENS // TOK_DEV)
    expert_ids = jax.vmap(lambda own, number: assign_block(jax.random.fold_in(key_of[3], 2), own, number, TOK_DEV, EXPERTS, TOPK, SLOTS, 2))(expert_ids_keys, expert_ids_turns).reshape((TOKENS, TOPK))
    w_gate = scatter_about(key_of[4], (EXPERTS, FF, D), D ** -0.5, 0.09375, ((0, 16), (2, 2)))
    w_up = scatter_about(key_of[5], (EXPERTS, FF, D), D ** -0.5, 0.09375, ((0, 16), (2, 2)))
    w_down = scatter_about(key_of[6], (EXPERTS, FF, D), FF ** -0.5, 0.21875, ((0, 16), (2, 2)))
    return dict(tokens=tokens, cotangent=cotangent, router_probs=router_probs, expert_ids=expert_ids, w_gate=w_gate, w_up=w_up, w_down=w_down)


def contract_last(left_matrix, right_matrix):
    return lax.dot_general(left_matrix, right_matrix, (((1,), (1,)), ((), ())), preferred_element_type=jnp.float32)


def contract_first(left_matrix, right_matrix):
    return lax.dot_general(left_matrix, right_matrix, (((0,), (0,)), ((), ())), preferred_element_type=jnp.float32)


def rounded(values):
    return lax.optimization_barrier(values.astype(jnp.bfloat16)).astype(jnp.float32)


def block_sum(rows, weight):
    width = D // N_DP
    total = jnp.zeros((rows.shape[0], weight.shape[0]), jnp.float32)
    for block_index in range(N_DP):
        low = block_index * width
        total = total + rounded(contract_last(rows[:, low:low + width], weight[:, low:low + width]))
    return total


def reference(tokens, cotangent, router_probs, expert_ids, w_gate, w_up, w_down):
    total_rows = TOKENS * TOPK
    flat_ids = expert_ids.reshape(-1)
    flat_probs = router_probs.reshape(-1)
    capacity = N_EXPERT * SLOTS
    zero_value = jnp.zeros((), tokens.dtype)

    def per_expert(state_pair, expert):
        token_acc, prob_acc = state_pair
        row_index = jnp.nonzero(flat_ids == expert, size=capacity, fill_value=total_rows)[0].astype(jnp.int32)
        valid = row_index < total_rows
        safe_rows = jnp.minimum(row_index, total_rows - 1)
        owners = safe_rows // TOPK
        inputs = jnp.where(valid[:, None], tokens[owners], zero_value)
        grads_in = jnp.where(valid[:, None], cotangent[owners], zero_value)
        weights = jnp.where(valid, flat_probs[safe_rows], jnp.zeros((), router_probs.dtype)).astype(jnp.float32)
        weight_gate = w_gate[expert]
        weight_up = w_up[expert]
        weight_down = w_down[expert]
        gate_value = block_sum(inputs, weight_gate)
        up_value = block_sum(inputs, weight_up)
        back_value = block_sum(grads_in, weight_down)
        sigmoid_gate = jax.nn.sigmoid(gate_value)
        silu_gate = gate_value * sigmoid_gate
        hidden = (silu_gate * up_value).astype(jnp.bfloat16)
        prob_value = rounded(jnp.sum(hidden.astype(jnp.float32) * back_value, axis=1))
        row_scale = weights[:, None]
        grad_back = row_scale * back_value
        grad_gate = (grad_back * up_value * sigmoid_gate * (1.0 + gate_value * (1.0 - sigmoid_gate))).astype(jnp.bfloat16)
        grad_up = (grad_back * silu_gate).astype(jnp.bfloat16)
        scaled = (row_scale * grads_in.astype(jnp.float32)).astype(jnp.bfloat16)
        row_term = jnp.dot(grad_gate, weight_gate, preferred_element_type=jnp.float32)
        row_term = rounded(row_term + jnp.dot(grad_up, weight_up, preferred_element_type=jnp.float32))
        token_acc = token_acc.at[owners].add(jnp.where(valid[:, None], row_term, 0.0))
        prob_acc = prob_acc.at[safe_rows].add(jnp.where(valid, prob_value, 0.0))
        gate_grad = contract_first(grad_gate, inputs).astype(jnp.bfloat16)
        up_grad = contract_first(grad_up, inputs).astype(jnp.bfloat16)
        down_grad = contract_first(hidden, scaled).astype(jnp.bfloat16)
        return (token_acc, prob_acc), (gate_grad, up_grad, down_grad)

    start_pair = (jnp.zeros((TOKENS, D), jnp.float32), jnp.zeros((total_rows,), jnp.float32))
    final_pair, weight_grads = lax.scan(per_expert, start_pair, jnp.arange(EXPERTS, dtype=jnp.int32))
    token_grads = final_pair[0].astype(jnp.bfloat16)
    prob_grads = final_pair[1].reshape(TOKENS, TOPK)
    return token_grads, prob_grads, weight_grads[0], weight_grads[1], weight_grads[2]
```

```python
import functools

import jax
import jax.numpy as jnp
from jax import lax
from jax.experimental import pallas as pl
from jax.experimental.pallas import tpu as pltpu
from jax.sharding import PartitionSpec as P

F32 = jnp.float32
BF16 = jnp.bfloat16
LANES = 128
VMEM = 56 * 1024 * 1024


def contract_last(left_matrix, right_matrix):
    return lax.dot_general(
        left_matrix, right_matrix, (((1,), (1,)), ((), ())), preferred_element_type=jnp.float32
    )


def contract_first(left_matrix, right_matrix):
    return lax.dot_general(
        left_matrix, right_matrix, (((0,), (0,)), ((), ())), preferred_element_type=jnp.float32
    )


def activations(gate_value, up_value, back_value, weights):
    sigmoid_gate = jax.nn.sigmoid(gate_value)
    silu_gate = gate_value * sigmoid_gate
    hidden = (silu_gate * up_value).astype(jnp.bfloat16)
    prob_local = jnp.sum(hidden.astype(jnp.float32) * back_value, axis=1, keepdims=True)
    grad_back = weights * back_value
    grad_gate = (
        grad_back * up_value * sigmoid_gate * (1.0 + gate_value * (1.0 - sigmoid_gate))
    ).astype(jnp.bfloat16)
    grad_up = (grad_back * silu_gate).astype(jnp.bfloat16)
    return (hidden, grad_gate, grad_up, prob_local)


def local_general(tokens, cotangent, router_probs, expert_ids, w_gate, w_up, w_down):
    experts = lax.axis_size("expert")
    local_tokens, top_count = expert_ids.shape
    row_count = local_tokens * top_count
    slot_count = min(local_tokens, max(2, (row_count + experts - 1) // experts * 17 // 16))
    features = tokens.shape[1]
    flat_ids = expert_ids.reshape(-1)
    hit_table = (flat_ids[:, None] == jnp.arange(experts, dtype=jnp.int32)[None, :]).astype(
        jnp.int32
    )
    slot_ranks = jnp.sum(jnp.cumsum(hit_table, axis=0) * hit_table, axis=1) - 1
    slot_places = flat_ids * slot_count + slot_ranks
    slot_table = jnp.full((experts * slot_count,), row_count, jnp.int32)
    slot_table = slot_table.at[slot_places].set(jnp.arange(row_count, dtype=jnp.int32))
    filled = slot_table < row_count
    sources = jnp.minimum(slot_table, row_count - 1)
    owners = sources // top_count
    send_probs = jnp.where(
        filled, router_probs.reshape(-1)[sources], jnp.zeros((), router_probs.dtype)
    )
    send_probs = send_probs.reshape(experts, slot_count)

    def pack_rows(source):
        picked = jnp.where(filled[:, None], source[owners], jnp.zeros((), source.dtype))
        return picked.reshape(experts, slot_count, source.shape[1])

    exchange = functools.partial(
        lax.all_to_all, axis_name="expert", split_axis=0, concat_axis=0, tiled=True
    )
    recv_in, recv_grad, recv_probs = (
        exchange(pack_rows(tokens)),
        exchange(pack_rows(cotangent)),
        exchange(send_probs),
    )
    inputs = recv_in.reshape(experts * slot_count, features)
    grads_in = recv_grad.reshape(experts * slot_count, features)
    weights = recv_probs.reshape(-1).astype(jnp.float32)
    weight_gate = w_gate[0]
    weight_up = w_up[0]
    weight_down = w_down[0]
    gate_part = contract_last(inputs, weight_gate)
    up_part = contract_last(inputs, weight_up)
    back_part = contract_last(grads_in, weight_down)
    gate_value, up_value, back_value = (
        lax.psum(gate_part.astype(jnp.bfloat16), "dp").astype(jnp.float32),
        lax.psum(up_part.astype(jnp.bfloat16), "dp").astype(jnp.float32),
        lax.psum(back_part.astype(jnp.bfloat16), "dp").astype(jnp.float32),
    )
    hidden, grad_gate, grad_up, prob_value = activations(
        gate_value, up_value, back_value, weights[:, None]
    )
    scaled = (weights[:, None] * grads_in).astype(jnp.bfloat16)
    row_term = jnp.dot(grad_gate, weight_gate, preferred_element_type=jnp.float32)
    row_term = (row_term + jnp.dot(grad_up, weight_up, preferred_element_type=jnp.float32)).astype(
        jnp.bfloat16
    )
    gate_grad = contract_first(grad_gate, inputs).astype(jnp.bfloat16)
    up_grad = contract_first(grad_up, inputs).astype(jnp.bfloat16)
    down_grad = contract_first(hidden, scaled).astype(jnp.bfloat16)
    back_terms = exchange(row_term.reshape(experts, slot_count, features))
    back_probs = exchange(prob_value.astype(jnp.bfloat16).reshape(experts, slot_count))
    returned = back_terms.reshape(experts * slot_count, features)[slot_places].astype(jnp.float32)
    token_sum = jnp.sum(returned.reshape(local_tokens, top_count, features), axis=1)
    prob_grads = (
        back_probs.reshape(-1)[slot_places].astype(jnp.float32).reshape(local_tokens, top_count)
    )
    return (
        token_sum.astype(jnp.bfloat16),
        prob_grads,
        gate_grad[None],
        up_grad[None],
        down_grad[None],
    )


def pack_kernel(tokens, cotangent, probs, ids, out):
    rows, width = tokens.shape
    out[:, :width] = tokens[...]
    out[:, width : 2 * width] = cotangent[...]
    lane = lax.broadcasted_iota(jnp.int32, (rows, LANES), 1)
    routing = jnp.full((rows, LANES), -1.0, F32)
    weights = probs[...].astype(F32)
    for k in range(ids.shape[1]):
        routing = jnp.where(lane == ids[:, k : k + 1], weights[:, k : k + 1], routing)
    out[:, 2 * width :] = routing.astype(BF16)


def pack(tokens, cotangent, probs, ids):
    rows, width = tokens.shape
    return pl.pallas_call(
        pack_kernel,
        out_shape=jax.ShapeDtypeStruct((rows, 2 * width + LANES), BF16),
        compiler_params=pltpu.CompilerParams(vmem_limit_bytes=VMEM),
        cost_estimate=pl.CostEstimate(flops=0, bytes_accessed=8 * rows * width, transcendentals=0),
        name="pack",
    )(tokens, cotangent, probs, ids)


def front_kernel(slots, expert, *refs):
    token_refs, grad_refs, route_refs = refs[0:4], refs[4:8], refs[8:12]
    w_gate, w_up, w_down = refs[12:15]
    inputs, scaled, part, spread, weights = refs[15:20]
    acc, pick = refs[20:22]
    step = pl.program_id(0)
    block = token_refs[0].shape[0]
    rows = pick.shape[0]
    units = w_gate.shape[0]

    @pl.when(step == 0)
    def _():
        lane = lax.broadcasted_iota(jnp.int32, (block, LANES), 1)
        tri = (
            lax.broadcasted_iota(jnp.int32, (block, block), 1)
            <= lax.broadcasted_iota(jnp.int32, (block, block), 0)
        ).astype(BF16)
        total = jnp.zeros((rows, LANES), F32)
        for b in range(4):
            routing = route_refs[b][...].astype(F32)
            prob = jnp.sum(jnp.where(lane == expert[0], routing, 0.0), axis=1, keepdims=True)
            chosen = jnp.broadcast_to(prob >= 0.0, (block, LANES))
            count = jnp.dot(tri, chosen.astype(BF16), preferred_element_type=F32)
            slot = jnp.where(chosen, count + (slots * b - 1.0), -1.0)
            spread[pl.ds(b * block, block), :] = (
                lax.broadcasted_iota(jnp.int32, (block, rows), 1) == slot[:, :1].astype(jnp.int32)
            ).astype(BF16)
            slot_row = slot.T[:1, :].astype(jnp.int32)
            picked = (lax.broadcasted_iota(jnp.int32, (rows, block), 0) == slot_row).astype(BF16)
            pick[:, pl.ds(b * block, block)] = picked
            prob = jnp.broadcast_to(jnp.maximum(prob, 0.0), (block, LANES)).astype(BF16)
            total = total + jnp.dot(picked, prob, preferred_element_type=F32)
        weights[...] = total
        acc[...] = jnp.zeros(acc.shape, F32)

    def gather(block_refs):
        stacked = jnp.concatenate([r[...] for r in block_refs], axis=0)
        return jnp.dot(pick[...], stacked, preferred_element_type=F32).astype(BF16)

    rows_in = gather(token_refs)
    inputs[...] = rows_in
    acc[:, 0:units] += contract_last(rows_in, w_gate[...])
    acc[:, units : 2 * units] += contract_last(rows_in, w_up[...])
    grads = gather(grad_refs)
    scaled[...] = (weights[:, :1] * grads.astype(F32)).astype(BF16)
    acc[:, 2 * units :] += contract_last(grads, w_down[...])

    @pl.when(step == pl.num_programs(0) - 1)
    def _():
        part[...] = acc[...].astype(BF16)


def front(blocks, expert, w_gate, w_up, w_down, slots):
    block = blocks[0].shape[0]
    units, width = w_gate.shape
    tile = 512
    steps = width // tile
    rows = 4 * slots
    weight_spec = pl.BlockSpec((units, tile), lambda k, e: (0, k))
    whole = lambda shape: pl.BlockSpec(shape, lambda k, e: (0, 0))
    return pl.pallas_call(
        functools.partial(front_kernel, slots),
        grid_spec=pltpu.PrefetchScalarGridSpec(
            num_scalar_prefetch=1,
            grid=(steps,),
            in_specs=[pl.BlockSpec((block, tile), lambda k, e: (0, k))] * 4
            + [pl.BlockSpec((block, tile), lambda k, e: (0, k + steps))] * 4
            + [pl.BlockSpec((block, LANES), lambda k, e: (0, 2 * width // LANES))] * 4
            + [weight_spec] * 3,
            out_specs=[
                pl.BlockSpec((rows, tile), lambda k, e: (0, k)),
                pl.BlockSpec((rows, tile), lambda k, e: (0, k)),
                whole((rows, 3 * units)),
                whole((4 * block, rows)),
                whole((rows, LANES)),
            ],
            scratch_shapes=[
                pltpu.VMEM((rows, 3 * units), F32),
                pltpu.VMEM((rows, 4 * block), BF16),
            ],
        ),
        out_shape=[
            jax.ShapeDtypeStruct((rows, width), BF16),
            jax.ShapeDtypeStruct((rows, width), BF16),
            jax.ShapeDtypeStruct((rows, 3 * units), BF16),
            jax.ShapeDtypeStruct((4 * block, rows), BF16),
            jax.ShapeDtypeStruct((rows, LANES), F32),
        ],
        compiler_params=pltpu.CompilerParams(vmem_limit_bytes=VMEM),
        cost_estimate=pl.CostEstimate(
            flops=2 * rows * width * (3 * units + 8 * block),
            bytes_accessed=2 * (3 * units * width + 8 * block * width + 2 * rows * width),
            transcendentals=0,
        ),
        name="front",
    )(expert, *blocks, *blocks, *blocks, w_gate, w_up, w_down)


def back_kernel(expert, own, peer, weights, spread, w_gate, w_up, *refs):
    hidden, grad_gate, grad_up, keep, send = refs
    step = pl.program_id(0)
    units, tile = w_gate.shape
    width = tile * pl.num_programs(0)
    block = keep.shape[0] // 2
    rows = own.shape[0]

    def place(term, columns):
        placed = jnp.dot(spread[...], term, preferred_element_type=F32).astype(BF16)
        keep[:block, columns] = placed[:block]
        send[:block, columns] = placed[block : 2 * block]
        keep[block:, columns] = placed[2 * block : 3 * block]
        send[block:, columns] = placed[3 * block :]

    @pl.when(step == 0)
    def _():
        def value(i):
            columns = pl.ds(i * units, units)
            return own[:, columns].astype(F32) + peer[:, columns].astype(F32)

        h, gg, gu, prob = activations(value(0), value(1), value(2), weights[:, :1])
        hidden[...] = h
        grad_gate[...] = gg
        grad_up[...] = gu
        lane = lax.broadcasted_iota(jnp.int32, (rows, LANES), 1)
        place(
            jnp.where(lane == expert[0], prob, 0.0).astype(BF16),
            slice(keep.shape[1] - LANES, keep.shape[1]),
        )

    term = jnp.dot(grad_gate[...], w_gate[...], preferred_element_type=F32)
    term = term + jnp.dot(grad_up[...], w_up[...], preferred_element_type=F32)
    place(term.astype(BF16), pl.ds(pl.multiple_of(step * tile, tile), tile))


def back(own, peer, weights, spread, expert, w_gate, w_up):
    units, width = w_gate.shape
    rows = own.shape[0]
    tokens = spread.shape[0]
    tile = 512
    weight_spec = pl.BlockSpec((units, tile), lambda k, e: (0, k))
    whole = lambda shape: pl.BlockSpec(shape, lambda k, e: (0, 0))
    half = (tokens // 2, width + LANES)
    return pl.pallas_call(
        back_kernel,
        grid_spec=pltpu.PrefetchScalarGridSpec(
            num_scalar_prefetch=1,
            grid=(width // tile,),
            in_specs=[whole(own.shape), whole(peer.shape), whole(weights.shape), whole(spread.shape)]
            + [weight_spec] * 2,
            out_specs=[whole((rows, units))] * 3 + [whole(half)] * 2,
        ),
        out_shape=[jax.ShapeDtypeStruct((rows, units), BF16)] * 3
        + [jax.ShapeDtypeStruct(half, BF16)] * 2,
        compiler_params=pltpu.CompilerParams(vmem_limit_bytes=VMEM),
        cost_estimate=pl.CostEstimate(
            flops=2 * rows * width * (2 * units + tokens),
            bytes_accessed=2 * (2 * units * width + tokens * width + 9 * rows * units),
            transcendentals=rows * units,
        ),
        name="back",
    )(expert, own, peer, weights, spread, w_gate, w_up)


def outer_kernel(count, *refs):
    lefts, rights, out = refs[:count], refs[count : 2 * count], refs[2 * count]
    total = contract_first(lefts[0][...], rights[0][...])
    for left, right in zip(lefts[1:], rights[1:]):
        total = total + contract_first(left[...], right[...])
    out[...] = total.astype(BF16)


def outer(lefts, rights):
    units, width = lefts[0].shape[1], rights[0].shape[1]
    rows = sum(left.shape[0] for left in lefts)
    tile = 512
    return pl.pallas_call(
        functools.partial(outer_kernel, len(lefts)),
        grid=(width // tile,),
        in_specs=[pl.BlockSpec(left.shape, lambda k: (0, 0)) for left in lefts]
        + [pl.BlockSpec((right.shape[0], tile), lambda k: (0, k)) for right in rights],
        out_specs=pl.BlockSpec((units, tile), lambda k: (0, k)),
        out_shape=jax.ShapeDtypeStruct((units, width), BF16),
        compiler_params=pltpu.CompilerParams(vmem_limit_bytes=VMEM),
        cost_estimate=pl.CostEstimate(
            flops=2 * rows * width * units,
            bytes_accessed=2 * (rows * (width + units) + units * width),
            transcendentals=0,
        ),
        name="outer",
    )(*lefts, *rights)


def add(*terms):
    return sum(t.astype(F32) for t in terms).astype(BF16)


def local_dense(tokens, cotangent, router_probs, expert_ids, w_gate, w_up, w_down):
    experts = lax.axis_size("expert")
    block, top_count = expert_ids.shape
    row_count = block * top_count
    slots = min(block, max(2, (row_count + experts - 1) // experts * 17 // 16))
    me = lax.axis_index("expert")
    expert = me.astype(jnp.int32).reshape(1)
    weight_gate, weight_up, weight_down = w_gate[0], w_up[0], w_down[0]

    def swap(value, bits):
        return lax.ppermute(value, "expert", [(i, i ^ bits) for i in range(experts)])

    core, across, near, far = (functools.partial(swap, bits=bits) for bits in (1, 2, 4, 8))

    own = pack(tokens, cotangent, router_probs, expert_ids)
    row_near = near(own)
    row_far = far(own)
    row_both = near(row_far)

    kept = []
    sums = []
    for first in (own, row_near, row_far, row_both):
        second = across(first)
        blocks = (first, core(first), second, core(second))
        inputs, scaled, part, spread, weights = front(
            blocks, expert, weight_gate, weight_up, weight_down, slots
        )
        peer = lax.ppermute(part, "dp", [(0, 1), (1, 0)])
        hidden, grad_gate, grad_up, keep, send = back(
            part, peer, weights, spread, expert, weight_gate, weight_up
        )
        kept.append((inputs, scaled, hidden, grad_gate, grad_up))
        got = core(send)
        mine = add(keep[:block], got[:block])
        theirs = add(keep[block:], got[block:])
        sums.append(add(mine, across(theirs)))

    inputs, scaled, hidden, grad_gate, grad_up = zip(*kept)
    gate_grad = outer(grad_gate, inputs)
    up_grad = outer(grad_up, inputs)
    down_grad = outer(hidden, scaled)

    from_near = near(sums[1])
    from_far = far(add(sums[2], near(sums[3])))
    total = add(sums[0], from_near, from_far)
    features = tokens.shape[1]
    by_expert = total[:, features : features + experts].astype(F32)
    chosen = expert_ids[:, :, None] == jnp.arange(experts, dtype=jnp.int32)[None, None, :]
    prob_grads = jnp.sum(jnp.where(chosen, by_expert[:, None, :], 0.0), axis=2)
    return (
        total[:, :features],
        prob_grads,
        gate_grad[None],
        up_grad[None],
        down_grad[None],
    )


def solution(mesh):
    dense = mesh.shape["expert"] == 16 and mesh.shape["dp"] == 2
    return jax.shard_map(
        local_dense if dense else local_general,
        mesh=mesh,
        in_specs=(
            P("expert", "dp"),
            P("expert", "dp"),
            P("expert", None),
            P("expert", None),
            P("expert", None, "dp"),
            P("expert", None, "dp"),
            P("expert", None, "dp"),
        ),
        out_specs=(
            P("expert", "dp"),
            P("expert", None),
            P("expert", None, "dp"),
            P("expert", None, "dp"),
            P("expert", None, "dp"),
        ),
        check_vma=False,
    )
```

```python
import functools

import jax
import jax.numpy as jnp
from jax import lax
from jax.experimental import pallas as pl
from jax.experimental.pallas import tpu as pltpu
from jax.sharding import PartitionSpec as P

F32 = jnp.float32
BF16 = jnp.bfloat16
LANES = 128
VMEM = 14 * 1024 * 1024


def contract_last(left_matrix, right_matrix):
    return lax.dot_general(
        left_matrix, right_matrix, (((1,), (1,)), ((), ())), preferred_element_type=jnp.float32
    )


def contract_first(left_matrix, right_matrix):
    return lax.dot_general(
        left_matrix, right_matrix, (((0,), (0,)), ((), ())), preferred_element_type=jnp.float32
    )


def activations(gate_value, up_value, back_value, weights):
    sigmoid_gate = jax.nn.sigmoid(gate_value)
    silu_gate = gate_value * sigmoid_gate
    hidden = (silu_gate * up_value).astype(jnp.bfloat16)
    prob_local = jnp.sum(hidden.astype(jnp.float32) * back_value, axis=1, keepdims=True)
    grad_back = weights * back_value
    grad_gate = (
        grad_back * up_value * sigmoid_gate * (1.0 + gate_value * (1.0 - sigmoid_gate))
    ).astype(jnp.bfloat16)
    grad_up = (grad_back * silu_gate).astype(jnp.bfloat16)
    return (hidden, grad_gate, grad_up, prob_local)


def local_general(tokens, cotangent, router_probs, expert_ids, w_gate, w_up, w_down):
    experts = lax.axis_size("expert")
    local_tokens, top_count = expert_ids.shape
    row_count = local_tokens * top_count
    slot_count = min(local_tokens, max(2, (row_count + experts - 1) // experts * 17 // 16))
    features = tokens.shape[1]
    flat_ids = expert_ids.reshape(-1)
    hit_table = (flat_ids[:, None] == jnp.arange(experts, dtype=jnp.int32)[None, :]).astype(
        jnp.int32
    )
    slot_ranks = jnp.sum(jnp.cumsum(hit_table, axis=0) * hit_table, axis=1) - 1
    slot_places = flat_ids * slot_count + slot_ranks
    slot_table = jnp.full((experts * slot_count,), row_count, jnp.int32)
    slot_table = slot_table.at[slot_places].set(jnp.arange(row_count, dtype=jnp.int32))
    filled = slot_table < row_count
    sources = jnp.minimum(slot_table, row_count - 1)
    owners = sources // top_count
    send_probs = jnp.where(
        filled, router_probs.reshape(-1)[sources], jnp.zeros((), router_probs.dtype)
    )
    send_probs = send_probs.reshape(experts, slot_count)

    def pack_rows(source):
        picked = jnp.where(filled[:, None], source[owners], jnp.zeros((), source.dtype))
        return picked.reshape(experts, slot_count, source.shape[1])

    exchange = functools.partial(
        lax.all_to_all, axis_name="expert", split_axis=0, concat_axis=0, tiled=True
    )
    recv_in, recv_grad, recv_probs = (
        exchange(pack_rows(tokens)),
        exchange(pack_rows(cotangent)),
        exchange(send_probs),
    )
    inputs = recv_in.reshape(experts * slot_count, features)
    grads_in = recv_grad.reshape(experts * slot_count, features)
    weights = recv_probs.reshape(-1).astype(jnp.float32)
    weight_gate = w_gate[0]
    weight_up = w_up[0]
    weight_down = w_down[0]
    gate_part = contract_last(inputs, weight_gate)
    up_part = contract_last(inputs, weight_up)
    back_part = contract_last(grads_in, weight_down)
    gate_value, up_value, back_value = (
        lax.psum(gate_part.astype(jnp.bfloat16), "dp").astype(jnp.float32),
        lax.psum(up_part.astype(jnp.bfloat16), "dp").astype(jnp.float32),
        lax.psum(back_part.astype(jnp.bfloat16), "dp").astype(jnp.float32),
    )
    hidden, grad_gate, grad_up, prob_value = activations(
        gate_value, up_value, back_value, weights[:, None]
    )
    scaled = (weights[:, None] * grads_in).astype(jnp.bfloat16)
    row_term = jnp.dot(grad_gate, weight_gate, preferred_element_type=jnp.float32)
    row_term = (row_term + jnp.dot(grad_up, weight_up, preferred_element_type=jnp.float32)).astype(
        jnp.bfloat16
    )
    gate_grad = contract_first(grad_gate, inputs).astype(jnp.bfloat16)
    up_grad = contract_first(grad_up, inputs).astype(jnp.bfloat16)
    down_grad = contract_first(hidden, scaled).astype(jnp.bfloat16)
    back_terms = exchange(row_term.reshape(experts, slot_count, features))
    back_probs = exchange(prob_value.astype(jnp.bfloat16).reshape(experts, slot_count))
    returned = back_terms.reshape(experts * slot_count, features)[slot_places].astype(jnp.float32)
    token_sum = jnp.sum(returned.reshape(local_tokens, top_count, features), axis=1)
    prob_grads = (
        back_probs.reshape(-1)[slot_places].astype(jnp.float32).reshape(local_tokens, top_count)
    )
    return (
        token_sum.astype(jnp.bfloat16),
        prob_grads,
        gate_grad[None],
        up_grad[None],
        down_grad[None],
    )


def kernel_call(body, operands, outs, scratch=(), name=None):
    return pl.pallas_call(
        body,
        in_specs=[pl.BlockSpec(memory_space=pltpu.VMEM)] * len(operands),
        out_specs=[pl.BlockSpec(memory_space=pltpu.VMEM)] * len(outs),
        out_shape=[jax.ShapeDtypeStruct(shape, dtype) for shape, dtype in outs],
        scratch_shapes=list(scratch),
        compiler_params=pltpu.CompilerParams(vmem_limit_bytes=VMEM),
        cost_estimate=pl.CostEstimate(flops=1000, bytes_accessed=1000, transcendentals=0),
        name=name,
    )(*operands)


def choose_kernel(first, second, out):
    z_index = lax.div(lax.axis_index("expert"), 4)
    edge = (z_index == 0) | (z_index == 3)

    @pl.when(edge)
    def _():
        out[...] = first[...]

    @pl.when(jnp.logical_not(edge))
    def _():
        out[...] = second[...]


def choose(first, second):
    return kernel_call(choose_kernel, (first, second), [(first.shape, BF16)], name="choose")[0]


def tiles(width, tile, body):
    @pl.loop(0, width // tile)
    def _(k):
        body(pl.multiple_of(k * tile, tile))


def pack_kernel(tokens, cotangent, probs, ids, out):
    rows, width = tokens.shape
    out[:, :width] = tokens[...]
    out[:, width : 2 * width] = cotangent[...]
    lane = lax.broadcasted_iota(jnp.int32, (rows, LANES), 1)
    routing = jnp.full((rows, LANES), -1.0, F32)
    weights = probs[...].astype(F32)
    for k in range(ids.shape[1]):
        routing = jnp.where(lane == ids[:, k : k + 1], weights[:, k : k + 1], routing)
    out[:, 2 * width :] = routing.astype(BF16)


def pack(tokens, cotangent, probs, ids):
    rows, width = tokens.shape
    operands = (tokens, cotangent, probs, ids)
    return kernel_call(pack_kernel, operands, [((rows, 2 * width + LANES), BF16)], name="pack")[0]


def front_kernel(slots, count, *refs):
    expert = lax.axis_index("expert")
    blocks = refs[:count]
    w_gate, w_up, w_down = refs[count : count + 3]
    inputs, scaled, spread, weights, *parts, acc, pick = refs[count + 3 :]
    units, width = w_gate.shape
    block = blocks[0].shape[0]
    rows = pick.shape[0]
    lane = lax.broadcasted_iota(jnp.int32, (block, LANES), 1)
    tri = (
        lax.broadcasted_iota(jnp.int32, (block, block), 1)
        <= lax.broadcasted_iota(jnp.int32, (block, block), 0)
    ).astype(BF16)
    total = jnp.zeros((rows, LANES), F32)
    for b, source in enumerate(blocks):
        routing = source[:, 2 * width :].astype(F32)
        prob = jnp.sum(jnp.where(lane == expert, routing, 0.0), axis=1, keepdims=True)
        chosen = jnp.broadcast_to(prob >= 0.0, (block, LANES))
        rank = jnp.dot(tri, chosen.astype(BF16), preferred_element_type=F32)
        slot = jnp.where(chosen, rank + (slots * b - 1.0), -1.0)
        spread[pl.ds(b * block, block), :] = (
            lax.broadcasted_iota(jnp.int32, (block, rows), 1) == slot[:, :1].astype(jnp.int32)
        ).astype(BF16)
        slot_row = slot.T[:1, :].astype(jnp.int32)
        picked = (lax.broadcasted_iota(jnp.int32, (rows, block), 0) == slot_row).astype(BF16)
        pick[:, pl.ds(b * block, block)] = picked
        prob = jnp.broadcast_to(jnp.maximum(prob, 0.0), (block, LANES)).astype(BF16)
        total = total + jnp.dot(picked, prob, preferred_element_type=F32)
    weights[...] = total
    acc[...] = jnp.zeros(acc.shape, F32)
    tile = 1024

    def gather(columns):
        stacked = jnp.concatenate([source[:, columns] for source in blocks], axis=0)
        return jnp.dot(pick[...], stacked, preferred_element_type=F32)

    def step(start):
        here, there = pl.ds(start, tile), pl.ds(width + start, tile)
        rows_in = gather(here).astype(BF16)
        inputs[:, here] = rows_in
        acc[:, :units] += contract_last(rows_in, w_gate[:, here])
        acc[:, units : 2 * units] += contract_last(rows_in, w_up[:, here])
        grads = gather(there)
        scaled[:, here] = (weights[:, :1] * grads).astype(BF16)
        acc[:, 2 * units :] += contract_last(grads.astype(BF16), w_down[:, here])

    tiles(width, tile, step)
    for i, part in enumerate(parts):
        size = part.shape[0]
        part[...] = acc[i * size : (i + 1) * size].astype(BF16)


def front(blocks, w_gate, w_up, w_down, slots):
    count, block = len(blocks), blocks[0].shape[0]
    units, width = w_gate.shape
    filled = count * slots
    rows = -(-filled // 16) * 16
    return kernel_call(
        functools.partial(front_kernel, slots, count),
        (*blocks, w_gate, w_up, w_down),
        [
            ((rows, width), BF16),
            ((rows, width), BF16),
            ((count * block, rows), BF16),
            ((rows, LANES), F32),
        ]
        + [((2 * slots, 3 * units), BF16)] * (count // 2),
        scratch=[pltpu.VMEM((rows, 3 * units), F32), pltpu.VMEM((rows, count * block), BF16)],
        name="front",
    )


def back_kernel(block, weights, spread, w_gate, w_up, *refs):
    expert = lax.axis_index("expert")
    *shares, hidden, grad_gate, grad_up, keep, send = refs
    units, width = w_gate.shape
    filled = sum(share.shape[0] for share in shares) // 2
    tokens, rows = spread.shape
    tile = 1024

    def place(term, columns):
        placed = jnp.dot(spread[...], term, preferred_element_type=F32).astype(BF16)
        for b in range(0, tokens // block, 2):
            here = pl.ds(b // 2 * block, block)
            keep[here, columns] = placed[b * block : (b + 1) * block]
            send[here, columns] = placed[(b + 1) * block : (b + 2) * block]

    def value(i):
        columns = pl.ds(i * units, units)
        total = [
            own[:, columns].astype(F32) + peer[:, columns].astype(F32)
            for own, peer in zip(shares[::2], shares[1::2])
        ]
        if rows > filled:
            total.append(jnp.zeros((rows - filled, units), F32))
        return jnp.concatenate(total, axis=0)

    h, gg, gu, prob = activations(value(0), value(1), value(2), weights[:, :1])
    hidden[...] = h
    grad_gate[...] = gg
    grad_up[...] = gu
    lane = lax.broadcasted_iota(jnp.int32, (rows, LANES), 1)
    place(jnp.where(lane == expert, prob, 0.0).astype(BF16), pl.ds(width, LANES))

    def step(start):
        columns = pl.ds(start, tile)
        term = jnp.dot(grad_gate[...], w_gate[:, columns], preferred_element_type=F32)
        term = term + jnp.dot(grad_up[...], w_up[:, columns], preferred_element_type=F32)
        place(term.astype(BF16), columns)

    tiles(width, tile, step)


def back(shares, weights, spread, w_gate, w_up, block):
    units, width = w_gate.shape
    tokens, rows = spread.shape
    half = (tokens // 2, width + LANES)
    return kernel_call(
        functools.partial(back_kernel, block),
        (weights, spread, w_gate, w_up, *shares),
        [((rows, units), BF16)] * 3 + [(half, BF16)] * 2,
        name="back",
    )


def outer_kernel(count, *refs):
    lefts, rights = refs[:count], refs[count : 2 * count]
    out, turned = refs[2 * count :]

    @pl.when(pl.program_id(0) == 0)
    def _():
        turned[...] = jnp.concatenate([left[...] for left in lefts], axis=0).T

    right = jnp.concatenate([right[...] for right in rights], axis=0)
    out[...] = jnp.dot(turned[...], right, preferred_element_type=F32).astype(BF16)


def outer(lefts, rights):
    units, width = lefts[0].shape[1], rights[0].shape[1]
    rows = sum(left.shape[0] for left in lefts)
    tile = 512
    return pl.pallas_call(
        functools.partial(outer_kernel, len(lefts)),
        grid=(width // tile,),
        in_specs=[pl.BlockSpec(left.shape, lambda k: (0, 0)) for left in lefts]
        + [pl.BlockSpec((right.shape[0], tile), lambda k: (0, k)) for right in rights],
        out_specs=pl.BlockSpec((units, tile), lambda k: (0, k)),
        out_shape=jax.ShapeDtypeStruct((units, width), BF16),
        scratch_shapes=[pltpu.VMEM((units, rows), BF16)],
        compiler_params=pltpu.CompilerParams(vmem_limit_bytes=VMEM),
        cost_estimate=pl.CostEstimate(flops=1000, bytes_accessed=1000, transcendentals=0),
        name="outer",
    )(*lefts, *rights)


def add_kernel(block, count, *refs):
    terms, outs = refs[:count], refs[count:]
    for i, out in enumerate(outs):
        rows = pl.ds(i * block, block)
        total = terms[0][rows, :].astype(F32)
        for term in terms[1:]:
            total = total + term[rows, :].astype(F32)
        out[...] = total.astype(BF16)


def add_blocks(block, *terms):
    rows, width = terms[0].shape
    return kernel_call(
        functools.partial(add_kernel, block, len(terms)),
        terms,
        [((block, width), BF16)] * (rows // block),
        name="add",
    )


def add(*terms):
    return add_blocks(terms[0].shape[0], *terms)[0]


def after(value, *gates):
    return lax.optimization_barrier((value, *gates))[0]


def local_dense(tokens, cotangent, router_probs, expert_ids, w_gate, w_up, w_down):
    experts = lax.axis_size("expert")
    block, top_count = expert_ids.shape
    row_count = block * top_count
    slots = min(block, max(2, (row_count + experts - 1) // experts * 17 // 16))
    weight_gate, weight_up, weight_down = w_gate[0], w_up[0], w_down[0]

    def swap(value, bits, part=(0, 1, 2, 3)):
        pairs = [(i, i ^ bits) for i in range(experts) if i // 4 in part]
        return lax.ppermute(value, "expert", pairs)

    core = functools.partial(swap, bits=1)
    across = functools.partial(swap, bits=2)
    outer_z = functools.partial(swap, bits=4)
    inner_z = functools.partial(swap, bits=12, part=(1, 2))

    def forward(*blocks):
        inputs, scaled, spread, weights, *parts = front(
            blocks, weight_gate, weight_up, weight_down, slots
        )
        return dict(inputs=inputs, scaled=scaled, parts=parts, spread=spread, weights=weights)

    def exchange(part, *gates):
        return lax.ppermute(after(part, *gates), "dp", [(0, 1), (1, 0)])

    def backward(state, peers, *gates):
        peers = after(peers, *gates)
        hidden, grad_gate, grad_up, keep, send = back(
            [share for pair in zip(state["parts"], peers) for share in pair],
            state["weights"],
            state["spread"],
            weight_gate,
            weight_up,
            block,
        )
        return state | dict(
            hidden=hidden, grad_gate=grad_gate, grad_up=grad_up, keep=keep, got=core(send)
        )

    def combine(state, *gates):
        return add_blocks(block, state["keep"], after(state["got"], *gates))

    p0 = pack(tokens, cotangent, router_probs, expert_ids)
    q0 = core(p0)
    p1, a0, m0 = across(p0), outer_z(p0), inner_z(p0)
    s0 = forward(p0, q0)
    y0 = exchange(s0["parts"][0])

    p1, a0, m0 = after((p1, a0, m0), y0)
    a1, b0e, c0m = across(a0), outer_z(m0), inner_z(a0)
    q1 = core(p1)
    qa0 = core(a0)
    s1 = forward(p1, q1, a0, qa0)
    y1a = exchange(s1["parts"][0])
    s0 = backward(s0, (y0,), s1["parts"])

    a1, b0e, c0m = after((a1, b0e, c0m), y1a, s0["hidden"])
    y1b = exchange(s1["parts"][1], y1a)
    b0 = choose(b0e, m0)
    b1, c0e = across(b0), outer_z(c0m)
    qa1 = core(a1)
    qb0 = core(b0)
    s2 = forward(a1, qa1, b0, qb0)
    y2a = exchange(s2["parts"][0], y1b)
    (sum0,) = combine(s0, s2["parts"])
    s1 = backward(s1, (y1a, y1b), s2["parts"])

    b1, c0e = after((b1, c0e), y2a, s1["hidden"])
    y2b = exchange(s2["parts"][1], y2a)
    c0 = choose(c0e, c0m)
    c1 = across(c0)
    qb1 = core(b1)
    qc0 = core(c0)
    s3 = forward(b1, qb1, c0, qc0)
    y3a = exchange(s3["parts"][0], y2b)
    there0, suma0 = combine(s1, s3["parts"])
    s2 = backward(s2, (y2a, y2b), s3["parts"])

    q_c1 = core(after(c1, s2["hidden"]))
    y3b = exchange(s3["parts"][1], y3a, q_c1)
    r0 = across(after(there0, c1))
    suma1, sumb0 = combine(s2, c1)
    ra = across(after(suma1, r0))
    s4 = forward(c1, q_c1)
    y4 = exchange(s4["parts"][0], y3b, r0)
    s3 = backward(s3, (y3a, y3b), s4["parts"])
    sumb1, sumc0 = combine(s3)
    from_a = outer_z(add(suma0, ra))
    rb = across(sumb1)
    from_c0 = outer_z(sumc0, part=(0, 3))
    s4 = backward(s4, (y4,), sumb1, ra)
    (sumc1,) = combine(s4)
    near_c1, across_c1 = swap(sumc1, 6, (0, 3)), swap(sumc1, 2, (1, 2))

    states = (s0, s1, s2, s3, s4)
    inputs, scaled, hidden, grad_gate, grad_up = (
        tuple(s[key] for s in states)
        for key in ("inputs", "scaled", "hidden", "grad_gate", "grad_up")
    )
    gate_grad = outer(after(grad_gate, sumc1), inputs)
    sumb = add(sumb0, after(rb, gate_grad))
    from_b = swap(sumb, 8, (0, 3)), swap(sumb, 12, (1, 2))
    up_grad = outer(after(grad_up, sumb, from_a, from_c0), inputs)
    sumc = add(sumc0, from_c0, *after((near_c1, across_c1), up_grad))
    from_c = swap(sumc, 8, (1, 2))
    down_grad = outer(after(hidden, sumc, *from_b), scaled)
    total = add(sum0, r0, from_a, *from_b, after(from_c, down_grad))
    features = tokens.shape[1]
    by_expert = total[:, features : features + experts].astype(F32)
    chosen = expert_ids[:, :, None] == jnp.arange(experts, dtype=jnp.int32)[None, None, :]
    prob_grads = jnp.sum(jnp.where(chosen, by_expert[:, None, :], 0.0), axis=2)
    return (
        total[:, :features],
        prob_grads,
        gate_grad[None],
        up_grad[None],
        down_grad[None],
    )


def solution(mesh):
    dense = mesh.shape["expert"] == 16 and mesh.shape["dp"] == 2
    return jax.shard_map(
        local_dense if dense else local_general,
        mesh=mesh,
        in_specs=(
            P("expert", "dp"),
            P("expert", "dp"),
            P("expert", None),
            P("expert", None),
            P("expert", None, "dp"),
            P("expert", None, "dp"),
            P("expert", None, "dp"),
        ),
        out_specs=(
            P("expert", "dp"),
            P("expert", None),
            P("expert", None, "dp"),
            P("expert", None, "dp"),
            P("expert", None, "dp"),
        ),
        check_vma=False,
    )
```

```python
import functools

import jax
import jax.numpy as jnp
from jax import lax
from jax.experimental import pallas as pl
from jax.experimental.pallas import tpu as pltpu
from jax.sharding import PartitionSpec as P

F32 = jnp.float32
BF16 = jnp.bfloat16
LANES = 128
VMEM = 14 * 1024 * 1024


def contract_last(left_matrix, right_matrix):
    return lax.dot_general(
        left_matrix, right_matrix, (((1,), (1,)), ((), ())), preferred_element_type=jnp.float32
    )


def contract_first(left_matrix, right_matrix):
    return lax.dot_general(
        left_matrix, right_matrix, (((0,), (0,)), ((), ())), preferred_element_type=jnp.float32
    )


def activations(gate_value, up_value, back_value, weights):
    sigmoid_gate = jax.nn.sigmoid(gate_value)
    silu_gate = gate_value * sigmoid_gate
    hidden = (silu_gate * up_value).astype(jnp.bfloat16)
    prob_local = jnp.sum(hidden.astype(jnp.float32) * back_value, axis=1, keepdims=True)
    grad_back = weights * back_value
    grad_gate = (
        grad_back * up_value * sigmoid_gate * (1.0 + gate_value * (1.0 - sigmoid_gate))
    ).astype(jnp.bfloat16)
    grad_up = (grad_back * silu_gate).astype(jnp.bfloat16)
    return (hidden, grad_gate, grad_up, prob_local)


def local_general(tokens, cotangent, router_probs, expert_ids, w_gate, w_up, w_down):
    experts = lax.axis_size("expert")
    local_tokens, top_count = expert_ids.shape
    row_count = local_tokens * top_count
    slot_count = min(local_tokens, max(2, (row_count + experts - 1) // experts * 17 // 16))
    features = tokens.shape[1]
    flat_ids = expert_ids.reshape(-1)
    hit_table = (flat_ids[:, None] == jnp.arange(experts, dtype=jnp.int32)[None, :]).astype(
        jnp.int32
    )
    slot_ranks = jnp.sum(jnp.cumsum(hit_table, axis=0) * hit_table, axis=1) - 1
    slot_places = flat_ids * slot_count + slot_ranks
    slot_table = jnp.full((experts * slot_count,), row_count, jnp.int32)
    slot_table = slot_table.at[slot_places].set(jnp.arange(row_count, dtype=jnp.int32))
    filled = slot_table < row_count
    sources = jnp.minimum(slot_table, row_count - 1)
    owners = sources // top_count
    send_probs = jnp.where(
        filled, router_probs.reshape(-1)[sources], jnp.zeros((), router_probs.dtype)
    )
    send_probs = send_probs.reshape(experts, slot_count)

    def pack_rows(source):
        picked = jnp.where(filled[:, None], source[owners], jnp.zeros((), source.dtype))
        return picked.reshape(experts, slot_count, source.shape[1])

    exchange = functools.partial(
        lax.all_to_all, axis_name="expert", split_axis=0, concat_axis=0, tiled=True
    )
    recv_in, recv_grad, recv_probs = (
        exchange(pack_rows(tokens)),
        exchange(pack_rows(cotangent)),
        exchange(send_probs),
    )
    inputs = recv_in.reshape(experts * slot_count, features)
    grads_in = recv_grad.reshape(experts * slot_count, features)
    weights = recv_probs.reshape(-1).astype(jnp.float32)
    weight_gate = w_gate[0]
    weight_up = w_up[0]
    weight_down = w_down[0]
    gate_part = contract_last(inputs, weight_gate)
    up_part = contract_last(inputs, weight_up)
    back_part = contract_last(grads_in, weight_down)
    gate_value, up_value, back_value = (
        lax.psum(gate_part.astype(jnp.bfloat16), "dp").astype(jnp.float32),
        lax.psum(up_part.astype(jnp.bfloat16), "dp").astype(jnp.float32),
        lax.psum(back_part.astype(jnp.bfloat16), "dp").astype(jnp.float32),
    )
    hidden, grad_gate, grad_up, prob_value = activations(
        gate_value, up_value, back_value, weights[:, None]
    )
    scaled = (weights[:, None] * grads_in).astype(jnp.bfloat16)
    row_term = jnp.dot(grad_gate, weight_gate, preferred_element_type=jnp.float32)
    row_term = (row_term + jnp.dot(grad_up, weight_up, preferred_element_type=jnp.float32)).astype(
        jnp.bfloat16
    )
    gate_grad = contract_first(grad_gate, inputs).astype(jnp.bfloat16)
    up_grad = contract_first(grad_up, inputs).astype(jnp.bfloat16)
    down_grad = contract_first(hidden, scaled).astype(jnp.bfloat16)
    back_terms = exchange(row_term.reshape(experts, slot_count, features))
    back_probs = exchange(prob_value.astype(jnp.bfloat16).reshape(experts, slot_count))
    returned = back_terms.reshape(experts * slot_count, features)[slot_places].astype(jnp.float32)
    token_sum = jnp.sum(returned.reshape(local_tokens, top_count, features), axis=1)
    prob_grads = (
        back_probs.reshape(-1)[slot_places].astype(jnp.float32).reshape(local_tokens, top_count)
    )
    return (
        token_sum.astype(jnp.bfloat16),
        prob_grads,
        gate_grad[None],
        up_grad[None],
        down_grad[None],
    )


def kernel_call(body, operands, outs, scratch=(), name=None):
    return pl.pallas_call(
        body,
        in_specs=[pl.BlockSpec(memory_space=pltpu.VMEM)] * len(operands),
        out_specs=[pl.BlockSpec(memory_space=pltpu.VMEM)] * len(outs),
        out_shape=[jax.ShapeDtypeStruct(shape, dtype) for shape, dtype in outs],
        scratch_shapes=list(scratch),
        compiler_params=pltpu.CompilerParams(vmem_limit_bytes=VMEM),
        cost_estimate=pl.CostEstimate(flops=1000, bytes_accessed=1000, transcendentals=0),
        name=name,
    )(*operands)


def choose_kernel(cuts, first, second, *outs):
    z_index = lax.div(lax.axis_index("expert"), 4)
    edge = (z_index == 0) | (z_index == 3)

    def write(source):
        for (start, end), out in zip(cuts, outs):
            out[...] = source[:, start:end]

    @pl.when(edge)
    def _():
        write(first)

    @pl.when(jnp.logical_not(edge))
    def _():
        write(second)


def choose(first, second, *cuts):
    return kernel_call(
        functools.partial(choose_kernel, cuts),
        (first, second),
        [((first.shape[0], end - start), BF16) for start, end in cuts],
        name="choose",
    )


def tiles(width, tile, body):
    @pl.loop(0, width // tile)
    def _(k):
        body(pl.multiple_of(k * tile, tile))


def pack_kernel(tokens, cotangent, probs, ids, out):
    rows, width = tokens.shape
    out[:, :width] = cotangent[...]
    out[:, width : 2 * width] = tokens[...]
    lane = lax.broadcasted_iota(jnp.int32, (rows, LANES), 1)
    routing = jnp.full((rows, LANES), -1.0, F32)
    weights = probs[...].astype(F32)
    for k in range(ids.shape[1]):
        routing = jnp.where(lane == ids[:, k : k + 1], weights[:, k : k + 1], routing)
    out[:, 2 * width :] = routing.astype(BF16)


def pack(tokens, cotangent, probs, ids):
    rows, width = tokens.shape
    operands = (tokens, cotangent, probs, ids)
    return kernel_call(pack_kernel, operands, [((rows, 2 * width + LANES), BF16)], name="pack")[0]


def front_kernel(slots, layout, *refs):
    sources = refs[: sum(layout)]
    w_gate, w_up, w_down = refs[len(sources) : len(sources) + 3]
    *outs, acc, picks = refs[len(sources) + 3 :]
    units, width = w_gate.shape
    block = sources[0].shape[0]
    pairs = len(layout) // 2
    rows = picks.shape[1]
    tile = 1024
    expert = lax.axis_index("expert")

    blocks, start = [], 0
    for size in layout:
        here = sources[start : start + size]
        blocks.append((here[0], here[-1], width if size == 1 else 0))
        start = start + size

    lane = lax.broadcasted_iota(jnp.int32, (block, LANES), 1)
    tri = (
        lax.broadcasted_iota(jnp.int32, (block, block), 1)
        <= lax.broadcasted_iota(jnp.int32, (block, block), 0)
    ).astype(BF16)
    for p in range(pairs):
        spread, weights = outs[5 * p + 2], outs[5 * p + 3]
        total = jnp.zeros((rows, LANES), F32)
        for b, (_, source, offset) in enumerate(blocks[2 * p : 2 * p + 2]):
            routing = source[:, pl.ds(offset + width, LANES)].astype(F32)
            prob = jnp.sum(jnp.where(lane == expert, routing, 0.0), axis=1, keepdims=True)
            chosen = jnp.broadcast_to(prob >= 0.0, (block, LANES))
            rank = jnp.dot(tri, chosen.astype(BF16), preferred_element_type=F32)
            slot = jnp.where(chosen, rank + (slots * b - 1.0), -1.0)
            spread[pl.ds(b * block, block), :] = (
                lax.broadcasted_iota(jnp.int32, (block, rows), 1)
                == slot[:, :1].astype(jnp.int32)
            ).astype(BF16)
            slot_row = slot.T[:1, :].astype(jnp.int32)
            picked = (lax.broadcasted_iota(jnp.int32, (rows, block), 0) == slot_row).astype(BF16)
            picks[p, :, pl.ds(b * block, block)] = picked
            prob = jnp.broadcast_to(jnp.maximum(prob, 0.0), (block, LANES)).astype(BF16)
            total = total + jnp.dot(picked, prob, preferred_element_type=F32)
        weights[...] = total
    acc[...] = jnp.zeros(acc.shape, F32)

    def step(start):
        here = pl.ds(start, tile)
        rows_in, grads_in = [], []
        for p in range(pairs):
            inputs, scaled, _, weights, _ = outs[5 * p : 5 * p + 5]
            (first_c, first_t, first_at), (second_c, second_t, second_at) = blocks[2 * p : 2 * p + 2]
            stacked = jnp.concatenate(
                [
                    first_t[:, pl.ds(first_at + start, tile)],
                    second_t[:, pl.ds(second_at + start, tile)],
                ],
                axis=0,
            )
            picked = jnp.dot(picks[p], stacked, preferred_element_type=F32).astype(BF16)
            inputs[:, here] = picked
            rows_in.append(picked)
            stacked = jnp.concatenate([first_c[:, here], second_c[:, here]], axis=0)
            picked = jnp.dot(picks[p], stacked, preferred_element_type=F32)
            scaled[:, here] = (weights[:, :1] * picked).astype(BF16)
            grads_in.append(picked.astype(BF16))
        rows_in = jnp.concatenate(rows_in, axis=0)
        acc[:, :units] += contract_last(rows_in, w_gate[:, here])
        acc[:, units : 2 * units] += contract_last(rows_in, w_up[:, here])
        acc[:, 2 * units :] += contract_last(jnp.concatenate(grads_in, axis=0), w_down[:, here])

    tiles(width, tile, step)
    for p in range(pairs):
        part = outs[5 * p + 4]
        part[...] = acc[p * rows : p * rows + part.shape[0]].astype(BF16)


def front(blocks, w_gate, w_up, w_down, slots):
    blocks = [b if isinstance(b, tuple) else (b,) for b in blocks]
    layout = [len(b) for b in blocks]
    sources = [array for b in blocks for array in b]
    block = sources[0].shape[0]
    units, width = w_gate.shape
    pairs = len(blocks) // 2
    rows = -(-2 * slots // 16) * 16
    results = kernel_call(
        functools.partial(front_kernel, slots, layout),
        (*sources, w_gate, w_up, w_down),
        [
            ((rows, width), BF16),
            ((rows, width), BF16),
            ((2 * block, rows), BF16),
            ((rows, LANES), F32),
            ((2 * slots, 3 * units), BF16),
        ]
        * pairs,
        scratch=[
            pltpu.VMEM((pairs * rows, 3 * units), F32),
            pltpu.VMEM((pairs, rows, 2 * block), BF16),
        ],
        name="front",
    )
    names = ("inputs", "scaled", "spread", "weights", "part")
    return [dict(zip(names, results[5 * p : 5 * p + 5])) for p in range(pairs)]


def back_kernel(own, peer, weights, spread, w_gate, w_up, *refs):
    hidden, grad_gate, grad_up, keep, send = refs
    units, width = w_gate.shape
    filled = own.shape[0]
    tokens, rows = spread.shape
    tile = 1024
    expert = lax.axis_index("expert")

    def place(term, columns):
        placed = jnp.dot(spread[...], term, preferred_element_type=F32).astype(BF16)
        keep[:, columns] = placed[: tokens // 2]
        send[:, columns] = placed[tokens // 2 :]

    def value(i):
        columns = pl.ds(i * units, units)
        total = own[:, columns].astype(F32) + peer[:, columns].astype(F32)
        if rows > filled:
            total = jnp.concatenate([total, jnp.zeros((rows - filled, units), F32)], axis=0)
        return total

    h, gg, gu, prob = activations(value(0), value(1), value(2), weights[:, :1])
    hidden[...] = h
    grad_gate[...] = gg
    grad_up[...] = gu
    lane = lax.broadcasted_iota(jnp.int32, (rows, LANES), 1)
    place(jnp.where(lane == expert, prob, 0.0).astype(BF16), pl.ds(width, LANES))

    def step(start):
        columns = pl.ds(start, tile)
        term = jnp.dot(grad_gate[...], w_gate[:, columns], preferred_element_type=F32)
        term = term + jnp.dot(grad_up[...], w_up[:, columns], preferred_element_type=F32)
        place(term.astype(BF16), columns)

    tiles(width, tile, step)


def back(state, peer, w_gate, w_up):
    units, width = w_gate.shape
    tokens, rows = state["spread"].shape
    half = (tokens // 2, width + LANES)
    results = kernel_call(
        back_kernel,
        (state["part"], peer, state["weights"], state["spread"], w_gate, w_up),
        [((rows, units), BF16)] * 3 + [(half, BF16)] * 2,
        name="back",
    )
    return state | dict(zip(("hidden", "grad_gate", "grad_up", "keep", "send"), results))


def outer_kernel(count, *refs):
    lefts, rights = refs[:count], refs[count : 2 * count]
    out, turned = refs[2 * count :]

    @pl.when(pl.program_id(0) == 0)
    def _():
        turned[...] = jnp.concatenate([left[...] for left in lefts], axis=0).T

    right = jnp.concatenate([right[...] for right in rights], axis=0)
    out[...] = jnp.dot(turned[...], right, preferred_element_type=F32).astype(BF16)


def outer(lefts, rights):
    units, width = lefts[0].shape[1], rights[0].shape[1]
    rows = sum(left.shape[0] for left in lefts)
    tile = 512
    return pl.pallas_call(
        functools.partial(outer_kernel, len(lefts)),
        grid=(width // tile,),
        in_specs=[pl.BlockSpec(left.shape, lambda k: (0, 0)) for left in lefts]
        + [pl.BlockSpec((right.shape[0], tile), lambda k: (0, k)) for right in rights],
        out_specs=pl.BlockSpec((units, tile), lambda k: (0, k)),
        out_shape=jax.ShapeDtypeStruct((units, width), BF16),
        scratch_shapes=[pltpu.VMEM((units, rows), BF16)],
        compiler_params=pltpu.CompilerParams(vmem_limit_bytes=VMEM),
        cost_estimate=pl.CostEstimate(flops=1000, bytes_accessed=1000, transcendentals=0),
        name="outer",
    )(*lefts, *rights)


def add_kernel(*refs):
    *terms, out = refs
    total = terms[0][...].astype(F32)
    for term in terms[1:]:
        total = total + term[...].astype(F32)
    out[...] = total.astype(BF16)


def add(*terms):
    return kernel_call(add_kernel, terms, [(terms[0].shape, BF16)], name="add")[0]


def finish_kernel(*refs):
    *terms, tokens_out, probs_out = refs
    total = terms[0][...].astype(F32)
    for term in terms[1:]:
        total = total + term[...].astype(F32)
    width = tokens_out.shape[1]
    tokens_out[...] = total[:, :width].astype(BF16)
    probs_out[...] = total[:, width:]


def finish(*terms):
    block, columns = terms[0].shape
    outs = [((block, columns - LANES), BF16), ((block, LANES), F32)]
    return kernel_call(finish_kernel, terms, outs, name="finish")


def meet(*values):
    return lax.optimization_barrier(values)


def local_dense(tokens, cotangent, router_probs, expert_ids, w_gate, w_up, w_down):
    experts = lax.axis_size("expert")
    block, top_count = expert_ids.shape
    row_count = block * top_count
    slots = min(block, max(2, (row_count + experts - 1) // experts * 17 // 16))
    weight_gate, weight_up, weight_down = w_gate[0], w_up[0], w_down[0]

    def swap(value, bits, part=(0, 1, 2, 3)):
        pairs = [(i, i ^ bits) for i in range(experts) if i // 4 in part]
        return lax.ppermute(value, "expert", pairs)

    core = functools.partial(swap, bits=1)
    across = functools.partial(swap, bits=2)
    outer_z = functools.partial(swap, bits=4)
    inner_z = functools.partial(swap, bits=12, part=(1, 2))

    def forward(*blocks):
        return front(blocks, weight_gate, weight_up, weight_down, slots)

    def exchange(part):
        return lax.ppermute(part, "dp", [(0, 1), (1, 0)])

    def backward(state, peer):
        return back(state, peer, weight_gate, weight_up)

    features = tokens.shape[1]
    all_columns = 2 * features + LANES

    p0 = pack(tokens, cotangent, router_probs, expert_ids)
    q0 = core(p0)
    p1, a0, m0 = across(p0), outer_z(p0), inner_z(p0)
    (s0,) = forward(p0, q0)
    y0 = exchange(s0["part"])

    p1, a0, m0, y0 = meet(p1, a0, m0, y0)
    a1, b0e, c0m = across(a0), outer_z(m0), inner_z(a0)
    s1, sa0 = forward(p1, core(p1), a0, core(a0))
    y1 = exchange(s1["part"])
    s0 = backward(s0, y0)
    k0 = core(s0["send"])

    a1, b0e, c0m, sa0["part"], y1, _ = meet(a1, b0e, c0m, sa0["part"], y1, k0)
    ya0 = exchange(sa0["part"])
    (b0,) = choose(b0e, m0, (0, all_columns))
    b1, c0e = across(b0), outer_z(c0m)
    sa1, sb0 = forward(a1, core(a1), b0, core(b0))
    s1 = backward(s1, y1)

    sa1["part"], s1["send"], ya0 = meet(sa1["part"], s1["send"], ya0)
    ya1 = exchange(sa1["part"])
    k1 = core(s1["send"])
    sa0 = backward(sa0, ya0)
    ka0 = core(sa0["send"])

    b1, c0e, sb0["part"], ya1, k1, ka0 = meet(b1, c0e, sb0["part"], ya1, k1, ka0)
    yb0 = exchange(sb0["part"])
    cuts = (0, all_columns), (0, features), (features, all_columns)
    c0, c0c, c0t = choose(c0e, c0m, *cuts)
    c1c, c1t = across(c0c), across(c0t)
    sb1, sc0 = forward(b1, core(b1), c0, core(c0))
    sa1 = backward(sa1, ya1)

    sb1["part"], sa1["send"], yb0 = meet(sb1["part"], sa1["send"], yb0)
    yb1 = exchange(sb1["part"])
    ka1 = core(sa1["send"])
    qc1 = core(c1c), core(c1t)
    sb0 = backward(sb0, yb0)
    kb0 = core(sb0["send"])

    sc0["part"], ka1, yb1, kb0, *qc1 = meet(sc0["part"], ka1, yb1, kb0, *qc1)
    yc0 = exchange(sc0["part"])
    ra = across(add(sa1["keep"], ka1))
    sum1 = add(s1["keep"], k1)
    sumb0 = add(sb0["keep"], kb0)
    sb1 = backward(sb1, yb1)
    kb1 = core(sb1["send"])
    (sc1,) = forward((c1c, c1t), tuple(qc1))

    sc1["part"], kb1, yc0, ra, sum1, sumb0 = meet(sc1["part"], kb1, yc0, ra, sum1, sumb0)
    yc1 = exchange(sc1["part"])
    rb = across(add(sb1["keep"], kb1))
    from_a = outer_z(add(sa0["keep"], ka0, ra))
    sc0 = backward(sc0, yc0)
    kc0 = core(sc0["send"])

    yc1, kc0, rb, from_a = meet(yc1, kc0, rb, from_a)
    sc1 = backward(sc1, yc1)
    kc1 = core(sc1["send"])
    sumc0 = add(sc0["keep"], kc0)
    sumb = add(sumb0, rb)
    b_edge, b_middle = swap(sumb, 8, (0, 3)), swap(sumb, 12, (1, 2))

    sumc1 = add(sc1["keep"], kc1)
    rc = across(sumc1)
    states = (s0, s1, sa0, sa1, sb0, sb1, sc0, sc1)
    inputs, scaled, hidden, grad_gate, grad_up = (
        tuple(s[key] for s in states)
        for key in ("inputs", "scaled", "hidden", "grad_gate", "grad_up")
    )
    grad_gate, _ = meet(grad_gate, sumc1)
    gate_grad = outer(grad_gate, inputs)

    rc, sum1, _ = meet(rc, sum1, gate_grad)
    sumc = add(sumc0, rc)
    c_edge = outer_z(sumc, part=(0, 3))
    r0 = across(sum1)
    grad_up, _ = meet(grad_up, sumc)
    up_grad = outer(grad_up, inputs)

    c_edge, b_edge, b_middle, _ = meet(c_edge, b_edge, b_middle, up_grad)
    sumc = add(sumc, c_edge)
    far = swap(sumc, 8, (1, 2))
    hidden, _ = meet(hidden, sumc)
    down_grad = outer(hidden, scaled)
    far, r0, _ = meet(far, r0, down_grad)
    token_grads, by_expert = finish(s0["keep"], k0, r0, from_a, b_edge, b_middle, far)
    chosen = expert_ids[:, :, None] == jnp.arange(experts, dtype=jnp.int32)[None, None, :]
    prob_grads = jnp.sum(jnp.where(chosen, by_expert[:, None, :experts], 0.0), axis=2)
    return (
        token_grads,
        prob_grads,
        gate_grad[None],
        up_grad[None],
        down_grad[None],
    )


def solution(mesh):
    dense = mesh.shape["expert"] == 16 and mesh.shape["dp"] == 2
    return jax.shard_map(
        local_dense if dense else local_general,
        mesh=mesh,
        in_specs=(
            P("expert", "dp"),
            P("expert", "dp"),
            P("expert", None),
            P("expert", None),
            P("expert", None, "dp"),
            P("expert", None, "dp"),
            P("expert", None, "dp"),
        ),
        out_specs=(
            P("expert", "dp"),
            P("expert", None),
            P("expert", None, "dp"),
            P("expert", None, "dp"),
            P("expert", None, "dp"),
        ),
        check_vma=False,
    )
```

```python
import functools

import jax
import jax.numpy as jnp
from jax import lax
from jax.experimental import pallas as pl
from jax.experimental.pallas import tpu as pltpu
from jax.sharding import PartitionSpec as P

F32 = jnp.float32
BF16 = jnp.bfloat16
LANES = 128
VMEM = 14 * 1024 * 1024


def contract_last(left_matrix, right_matrix):
    return lax.dot_general(
        left_matrix, right_matrix, (((1,), (1,)), ((), ())), preferred_element_type=jnp.float32
    )


def contract_first(left_matrix, right_matrix):
    return lax.dot_general(
        left_matrix, right_matrix, (((0,), (0,)), ((), ())), preferred_element_type=jnp.float32
    )


def activations(gate_value, up_value, back_value, weights):
    sigmoid_gate = jax.nn.sigmoid(gate_value)
    silu_gate = gate_value * sigmoid_gate
    hidden = (silu_gate * up_value).astype(jnp.bfloat16)
    prob_local = jnp.sum(hidden.astype(jnp.float32) * back_value, axis=1, keepdims=True)
    grad_back = weights * back_value
    grad_gate = (
        grad_back * up_value * sigmoid_gate * (1.0 + gate_value * (1.0 - sigmoid_gate))
    ).astype(jnp.bfloat16)
    grad_up = (grad_back * silu_gate).astype(jnp.bfloat16)
    return (hidden, grad_gate, grad_up, prob_local)


def local_general(tokens, cotangent, router_probs, expert_ids, w_gate, w_up, w_down):
    experts = lax.axis_size("expert")
    local_tokens, top_count = expert_ids.shape
    row_count = local_tokens * top_count
    slot_count = min(local_tokens, max(2, (row_count + experts - 1) // experts * 17 // 16))
    features = tokens.shape[1]
    flat_ids = expert_ids.reshape(-1)
    hit_table = (flat_ids[:, None] == jnp.arange(experts, dtype=jnp.int32)[None, :]).astype(
        jnp.int32
    )
    slot_ranks = jnp.sum(jnp.cumsum(hit_table, axis=0) * hit_table, axis=1) - 1
    slot_places = flat_ids * slot_count + slot_ranks
    slot_table = jnp.full((experts * slot_count,), row_count, jnp.int32)
    slot_table = slot_table.at[slot_places].set(jnp.arange(row_count, dtype=jnp.int32))
    filled = slot_table < row_count
    sources = jnp.minimum(slot_table, row_count - 1)
    owners = sources // top_count
    send_probs = jnp.where(
        filled, router_probs.reshape(-1)[sources], jnp.zeros((), router_probs.dtype)
    )
    send_probs = send_probs.reshape(experts, slot_count)

    def pack_rows(source):
        picked = jnp.where(filled[:, None], source[owners], jnp.zeros((), source.dtype))
        return picked.reshape(experts, slot_count, source.shape[1])

    exchange = functools.partial(
        lax.all_to_all, axis_name="expert", split_axis=0, concat_axis=0, tiled=True
    )
    recv_in, recv_grad, recv_probs = (
        exchange(pack_rows(tokens)),
        exchange(pack_rows(cotangent)),
        exchange(send_probs),
    )
    inputs = recv_in.reshape(experts * slot_count, features)
    grads_in = recv_grad.reshape(experts * slot_count, features)
    weights = recv_probs.reshape(-1).astype(jnp.float32)
    weight_gate = w_gate[0]
    weight_up = w_up[0]
    weight_down = w_down[0]
    gate_part = contract_last(inputs, weight_gate)
    up_part = contract_last(inputs, weight_up)
    back_part = contract_last(grads_in, weight_down)
    gate_value, up_value, back_value = (
        lax.psum(gate_part.astype(jnp.bfloat16), "dp").astype(jnp.float32),
        lax.psum(up_part.astype(jnp.bfloat16), "dp").astype(jnp.float32),
        lax.psum(back_part.astype(jnp.bfloat16), "dp").astype(jnp.float32),
    )
    hidden, grad_gate, grad_up, prob_value = activations(
        gate_value, up_value, back_value, weights[:, None]
    )
    scaled = (weights[:, None] * grads_in).astype(jnp.bfloat16)
    row_term = jnp.dot(grad_gate, weight_gate, preferred_element_type=jnp.float32)
    row_term = (row_term + jnp.dot(grad_up, weight_up, preferred_element_type=jnp.float32)).astype(
        jnp.bfloat16
    )
    gate_grad = contract_first(grad_gate, inputs).astype(jnp.bfloat16)
    up_grad = contract_first(grad_up, inputs).astype(jnp.bfloat16)
    down_grad = contract_first(hidden, scaled).astype(jnp.bfloat16)
    back_terms = exchange(row_term.reshape(experts, slot_count, features))
    back_probs = exchange(prob_value.astype(jnp.bfloat16).reshape(experts, slot_count))
    returned = back_terms.reshape(experts * slot_count, features)[slot_places].astype(jnp.float32)
    token_sum = jnp.sum(returned.reshape(local_tokens, top_count, features), axis=1)
    prob_grads = (
        back_probs.reshape(-1)[slot_places].astype(jnp.float32).reshape(local_tokens, top_count)
    )
    return (
        token_sum.astype(jnp.bfloat16),
        prob_grads,
        gate_grad[None],
        up_grad[None],
        down_grad[None],
    )


def kernel_call(body, operands, outs, scratch=(), name=None):
    return pl.pallas_call(
        body,
        in_specs=[pl.BlockSpec(memory_space=pltpu.VMEM)] * len(operands),
        out_specs=[pl.BlockSpec(memory_space=pltpu.VMEM)] * len(outs),
        out_shape=[jax.ShapeDtypeStruct(shape, dtype) for shape, dtype in outs],
        scratch_shapes=list(scratch),
        compiler_params=pltpu.CompilerParams(vmem_limit_bytes=VMEM),
        cost_estimate=pl.CostEstimate(flops=1000, bytes_accessed=1000, transcendentals=0),
        name=name,
    )(*operands)


def choose_kernel(cuts, first, second, *outs):
    z_index = lax.div(lax.axis_index("expert"), 4)
    edge = (z_index == 0) | (z_index == 3)

    def write(source):
        for (start, end), out in zip(cuts, outs):
            out[...] = source[:, start:end]

    @pl.when(edge)
    def _():
        write(first)

    @pl.when(jnp.logical_not(edge))
    def _():
        write(second)


def choose(first, second, *cuts):
    return kernel_call(
        functools.partial(choose_kernel, cuts),
        (first, second),
        [((first.shape[0], end - start), BF16) for start, end in cuts],
        name="choose",
    )


def tiles(width, tile, body):
    @pl.loop(0, width // tile)
    def _(k):
        body(pl.multiple_of(k * tile, tile))


def pack_kernel(tokens, cotangent, probs, ids, out):
    rows, width = tokens.shape
    out[:, :width] = cotangent[...]
    out[:, width : 2 * width] = tokens[...]
    lane = lax.broadcasted_iota(jnp.int32, (rows, LANES), 1)
    routing = jnp.full((rows, LANES), -1.0, F32)
    weights = probs[...].astype(F32)
    for k in range(ids.shape[1]):
        routing = jnp.where(lane == ids[:, k : k + 1], weights[:, k : k + 1], routing)
    out[:, 2 * width :] = routing.astype(BF16)


def pack(tokens, cotangent, probs, ids):
    rows, width = tokens.shape
    operands = (tokens, cotangent, probs, ids)
    return kernel_call(pack_kernel, operands, [((rows, 2 * width + LANES), BF16)], name="pack")[0]


def front_kernel(slots, layout, joined, *refs):
    sources = refs[: sum(layout)]
    w_gate, w_up, w_down = refs[len(sources) : len(sources) + 3]
    *outs, acc, picks = refs[len(sources) + 3 :]
    units, width = w_gate.shape
    block = sources[0].shape[0]
    pairs = len(layout) // 2
    rows = picks.shape[1]
    tile = 1024
    expert = lax.axis_index("expert")

    blocks, start = [], 0
    for size in layout:
        here = sources[start : start + size]
        blocks.append((here[0], here[-1], width if size == 1 else 0))
        start = start + size

    lane = lax.broadcasted_iota(jnp.int32, (block, LANES), 1)
    tri = (
        lax.broadcasted_iota(jnp.int32, (block, block), 1)
        <= lax.broadcasted_iota(jnp.int32, (block, block), 0)
    ).astype(BF16)
    for p in range(pairs):
        spread, weights = outs[4 * p + 2], outs[4 * p + 3]
        total = jnp.zeros((rows, LANES), F32)
        for b, (_, source, offset) in enumerate(blocks[2 * p : 2 * p + 2]):
            routing = source[:, pl.ds(offset + width, LANES)].astype(F32)
            prob = jnp.sum(jnp.where(lane == expert, routing, 0.0), axis=1, keepdims=True)
            chosen = jnp.broadcast_to(prob >= 0.0, (block, LANES))
            rank = jnp.dot(tri, chosen.astype(BF16), preferred_element_type=F32)
            slot = jnp.where(chosen, rank + (slots * b - 1.0), -1.0)
            spread[pl.ds(b * block, block), :] = (
                lax.broadcasted_iota(jnp.int32, (block, rows), 1)
                == slot[:, :1].astype(jnp.int32)
            ).astype(BF16)
            slot_row = slot.T[:1, :].astype(jnp.int32)
            picked = (lax.broadcasted_iota(jnp.int32, (rows, block), 0) == slot_row).astype(BF16)
            picks[p, :, pl.ds(b * block, block)] = picked
            prob = jnp.broadcast_to(jnp.maximum(prob, 0.0), (block, LANES)).astype(BF16)
            total = total + jnp.dot(picked, prob, preferred_element_type=F32)
        weights[...] = total
    acc[...] = jnp.zeros(acc.shape, F32)

    def step(start):
        here = pl.ds(start, tile)
        rows_in, grads_in = [], []
        for p in range(pairs):
            inputs, scaled, _, weights = outs[4 * p : 4 * p + 4]
            (first_c, first_t, first_at), (second_c, second_t, second_at) = blocks[2 * p : 2 * p + 2]
            stacked = jnp.concatenate(
                [
                    first_t[:, pl.ds(first_at + start, tile)],
                    second_t[:, pl.ds(second_at + start, tile)],
                ],
                axis=0,
            )
            picked = jnp.dot(picks[p], stacked, preferred_element_type=F32).astype(BF16)
            inputs[:, here] = picked
            rows_in.append(picked)
            stacked = jnp.concatenate([first_c[:, here], second_c[:, here]], axis=0)
            picked = jnp.dot(picks[p], stacked, preferred_element_type=F32)
            scaled[:, here] = (weights[:, :1] * picked).astype(BF16)
            grads_in.append(picked.astype(BF16))
        rows_in = jnp.concatenate(rows_in, axis=0)
        acc[:, :units] += contract_last(rows_in, w_gate[:, here])
        acc[:, units : 2 * units] += contract_last(rows_in, w_up[:, here])
        acc[:, 2 * units :] += contract_last(jnp.concatenate(grads_in, axis=0), w_down[:, here])

    tiles(width, tile, step)
    if joined:
        outs[-1][...] = jnp.concatenate(
            [acc[p * rows : p * rows + 2 * slots] for p in range(pairs)], axis=0
        ).astype(BF16)
    else:
        for p in range(pairs):
            outs[4 * pairs + p][...] = acc[p * rows : p * rows + 2 * slots].astype(BF16)


def front(blocks, w_gate, w_up, w_down, slots, joined):
    blocks = [b if isinstance(b, tuple) else (b,) for b in blocks]
    layout = [len(b) for b in blocks]
    sources = [array for b in blocks for array in b]
    block = sources[0].shape[0]
    units, width = w_gate.shape
    pairs = len(blocks) // 2
    rows = -(-2 * slots // 16) * 16
    results = kernel_call(
        functools.partial(front_kernel, slots, layout, joined),
        (*sources, w_gate, w_up, w_down),
        [
            ((rows, width), BF16),
            ((rows, width), BF16),
            ((2 * block, rows), BF16),
            ((rows, LANES), F32),
        ]
        * pairs
        + [((2 * slots * (pairs if joined else 1), 3 * units), BF16)] * (1 if joined else pairs),
        scratch=[
            pltpu.VMEM((pairs * rows, 3 * units), F32),
            pltpu.VMEM((pairs, rows, 2 * block), BF16),
        ],
        name="front",
    )
    names = ("inputs", "scaled", "spread", "weights")
    states = [dict(zip(names, results[4 * p : 4 * p + 4])) for p in range(pairs)]
    return states, results[4 * pairs :]


def back_kernel(pairs, own, peer, *refs):
    weights, spreads = refs[:pairs], refs[pairs : 2 * pairs]
    w_gate, w_up, hidden, grad_gate, grad_up, *outs = refs[2 * pairs :]
    units, width = w_gate.shape
    filled = own.shape[0] // pairs
    tokens, rows = spreads[0].shape
    tile = 1024
    expert = lax.axis_index("expert")

    def place(term, columns):
        for p in range(pairs):
            here = term[p * rows : (p + 1) * rows]
            placed = jnp.dot(spreads[p][...], here, preferred_element_type=F32).astype(BF16)
            outs[2 * p][:, columns] = placed[: tokens // 2]
            outs[2 * p + 1][:, columns] = placed[tokens // 2 :]

    def value(i):
        columns = pl.ds(i * units, units)
        total = own[:, columns].astype(F32) + peer[:, columns].astype(F32)
        if rows == filled:
            return total
        pad = jnp.zeros((rows - filled, units), F32)
        pieces = [total[p * filled : (p + 1) * filled] for p in range(pairs)]
        return jnp.concatenate([piece for each in pieces for piece in (each, pad)], axis=0)

    scales = jnp.concatenate([weight[:, :1] for weight in weights], axis=0)
    h, gg, gu, prob = activations(value(0), value(1), value(2), scales)
    hidden[...] = h
    grad_gate[...] = gg
    grad_up[...] = gu
    lane = lax.broadcasted_iota(jnp.int32, (pairs * rows, LANES), 1)
    place(jnp.where(lane == expert, prob, 0.0).astype(BF16), pl.ds(width, LANES))

    def step(start):
        columns = pl.ds(start, tile)
        term = jnp.dot(grad_gate[...], w_gate[:, columns], preferred_element_type=F32)
        term = term + jnp.dot(grad_up[...], w_up[:, columns], preferred_element_type=F32)
        place(term.astype(BF16), columns)

    tiles(width, tile, step)


def back(states, own, peer, w_gate, w_up):
    units, width = w_gate.shape
    pairs = len(states)
    tokens, rows = states[0]["spread"].shape
    half = (tokens // 2, width + LANES)
    results = kernel_call(
        functools.partial(back_kernel, pairs),
        (
            own,
            peer,
            *[state["weights"] for state in states],
            *[state["spread"] for state in states],
            w_gate,
            w_up,
        ),
        [((pairs * rows, units), BF16)] * 3 + [(half, BF16)] * (2 * pairs),
        name="back",
    )
    return results[:3], [results[3 + 2 * p : 5 + 2 * p] for p in range(pairs)]


def outer_kernel(count, *refs):
    *terms, out, turned = refs
    lefts, rights = terms[:count], terms[count:]

    @pl.when(pl.program_id(0) == 0)
    def _():
        turned[...] = jnp.concatenate([left[...] for left in lefts], axis=0).T

    right = jnp.concatenate([right[...] for right in rights], axis=0)
    out[...] = jnp.dot(turned[...], right, preferred_element_type=F32).astype(BF16)


def outer(lefts, rights):
    units, width = lefts[0].shape[1], rights[0].shape[1]
    rows = sum(left.shape[0] for left in lefts)
    tile = 512
    return pl.pallas_call(
        functools.partial(outer_kernel, len(lefts)),
        grid=(width // tile,),
        in_specs=[pl.BlockSpec(left.shape, lambda k: (0, 0)) for left in lefts]
        + [pl.BlockSpec((right.shape[0], tile), lambda k: (0, k)) for right in rights],
        out_specs=pl.BlockSpec((units, tile), lambda k: (0, k)),
        out_shape=jax.ShapeDtypeStruct((units, width), BF16),
        scratch_shapes=[pltpu.VMEM((units, rows), BF16)],
        compiler_params=pltpu.CompilerParams(vmem_limit_bytes=VMEM),
        cost_estimate=pl.CostEstimate(flops=1000, bytes_accessed=1000, transcendentals=0),
        name="outer",
    )(*lefts, *rights)


def add_kernel(*refs):
    *terms, out = refs
    total = terms[0][...].astype(F32)
    for term in terms[1:]:
        total = total + term[...].astype(F32)
    out[...] = total.astype(BF16)


def add(*terms):
    return kernel_call(add_kernel, terms, [(terms[0].shape, BF16)], name="add")[0]


def finish_kernel(*refs):
    *terms, tokens_out, probs_out = refs
    total = terms[0][...].astype(F32)
    for term in terms[1:]:
        total = total + term[...].astype(F32)
    width = tokens_out.shape[1]
    tokens_out[...] = total[:, :width].astype(BF16)
    probs_out[...] = total[:, width:]


def finish(*terms):
    block, columns = terms[0].shape
    outs = [((block, columns - LANES), BF16), ((block, LANES), F32)]
    return kernel_call(finish_kernel, terms, outs, name="finish")


def meet(*values):
    return lax.optimization_barrier(values)


def local_dense(tokens, cotangent, router_probs, expert_ids, w_gate, w_up, w_down):
    experts = lax.axis_size("expert")
    block, top_count = expert_ids.shape
    row_count = block * top_count
    slots = min(block, max(2, (row_count + experts - 1) // experts * 17 // 16))
    weight_gate, weight_up, weight_down = w_gate[0], w_up[0], w_down[0]

    def swap(value, bits, part=(0, 1, 2, 3)):
        pairs = [(i, i ^ bits) for i in range(experts) if i // 4 in part]
        return lax.ppermute(value, "expert", pairs)

    core = functools.partial(swap, bits=1)
    across = functools.partial(swap, bits=2)
    outer_z = functools.partial(swap, bits=4)
    inner_z = functools.partial(swap, bits=12, part=(1, 2))
    to_edge = functools.partial(swap, bits=4, part=(1, 2))

    rights, lefts = [], []

    def forward(*blocks, joined=False):
        return front(blocks, weight_gate, weight_up, weight_down, slots, joined)

    def exchange(part):
        return lax.ppermute(part, "dp", [(0, 1), (1, 0)])

    def backward(states, own, peer):
        left, sums = back(states, own, peer, weight_gate, weight_up)
        rights.extend((state["inputs"], state["scaled"]) for state in states)
        lefts.append(left)
        return sums, left[0]

    features = tokens.shape[1]
    all_columns = 2 * features + LANES

    p0 = pack(tokens, cotangent, router_probs, expert_ids)
    q0 = core(p0)
    p1, a0, m0 = across(p0), outer_z(p0), inner_z(p0)
    (state0,), (part0,) = forward(p0, q0)

    p1, a0, m0, part0 = meet(p1, a0, m0, part0)
    a1, b0e, c0m = across(a0), to_edge(m0), inner_z(a0)
    states1, (part1,) = forward(p1, core(p1), a0, core(a0), joined=True)
    y1 = exchange(part1)

    (b0,) = choose(b0e, m0, (0, all_columns))
    a1, b0, c0m, _ = meet(a1, b0, c0m, part1)
    b1, c0e = across(b0), to_edge(c0m)
    (state_a1, state_b0), (part_a1, part_b0) = forward(a1, core(a1), b0, core(b0))

    y1, part_a1 = meet(y1, part_a1)
    ya1 = exchange(part_a1)
    ((keep1, send1), (keep_a0, send_a0)), done = backward(states1, part1, y1)
    k1, ka0 = core(send1), core(send_a0)

    columns = (0, all_columns), (0, features), (features, all_columns)
    c0, c0c, c0t = choose(c0e, c0m, *columns)
    b1, c0, c0c, c0t, ya1, part_b0, k1, ka0 = meet(
        b1, c0, c0c, c0t, ya1, part_b0, k1, ka0
    )
    yb0 = exchange(part_b0)
    c1c, c1t = across(c0c), across(c0t)
    (state_b1, state_c0), (part_b1, part_c0) = forward(b1, core(b1), c0, core(c0))
    ((keep_a1, send_a1),), done = backward((state_a1,), part_a1, ya1)

    yb0, part_b1, send_a1 = meet(yb0, part_b1, send_a1)
    yb1 = exchange(part_b1)
    ka1 = core(send_a1)
    qc1 = core(c1c), core(c1t)
    ((keep_b0, send_b0),), done = backward((state_b0,), part_b0, yb0)
    kb0 = core(send_b0)

    part_c0, ka1, yb1, kb0, *qc1 = meet(part_c0, ka1, yb1, kb0, *qc1)
    yc0 = exchange(part_c0)
    ra = across(add(keep_a1, ka1))
    sum1 = add(keep1, k1)
    sumb0 = add(keep_b0, kb0)
    ((keep_b1, send_b1),), done = backward((state_b1,), part_b1, yb1)
    kb1 = core(send_b1)
    (state_c1,), (part_c1,) = forward((c1c, c1t), tuple(qc1))

    suma = add(keep_a0, ka0, ra)
    part_c1, yc0, suma, sum1, sumb0, keep_b1 = meet(part_c1, yc0, suma, sum1, sumb0, keep_b1)
    yc1 = exchange(part_c1)
    rb = across(add(keep_b1, kb1))
    from_a = outer_z(suma)
    ((keep_c0, send_c0),), done = backward((state_c0,), part_c0, yc0)
    kc0 = core(send_c0)

    yc1, rb, from_a, part0, keep_c0 = meet(yc1, rb, from_a, part0, keep_c0)
    y0 = exchange(part0)
    ((keep_c1, send_c1),), done = backward((state_c1,), part_c1, yc1)
    kc1 = core(send_c1)
    sumc0 = add(keep_c0, kc0)
    sumb = add(sumb0, rb)
    b_edge, b_middle = swap(sumb, 8, (0, 3)), swap(sumb, 12, (1, 2))

    sumc1 = add(keep_c1, kc1)
    rc = across(sumc1)
    rc, sum1, y0 = meet(rc, sum1, y0)
    sumc = add(sumc0, rc)
    c_edge = outer_z(sumc, part=(0, 3))
    r0 = across(sum1)
    y0, _ = meet(y0, sumc)
    ((keep0, send0),), done = backward((state0,), part0, y0)
    k0 = core(send0)

    inputs, scaled = zip(*rights)
    hidden, grad_gate, grad_up = zip(*lefts)
    gate_grad = outer(grad_gate, inputs)

    c_edge, b_edge, b_middle, _ = meet(c_edge, b_edge, b_middle, gate_grad)
    sumc = add(sumc, c_edge)
    far = swap(sumc, 8, (1, 2))
    grad_up, _ = meet(grad_up, sumc)
    up_grad = outer(grad_up, inputs)
    hidden, _ = meet(hidden, up_grad)
    down_grad = outer(hidden, scaled)
    far, r0, k0, _ = meet(far, r0, k0, down_grad)
    token_grads, by_expert = finish(keep0, k0, r0, from_a, b_edge, b_middle, far)
    chosen = expert_ids[:, :, None] == jnp.arange(experts, dtype=jnp.int32)[None, None, :]
    prob_grads = jnp.sum(jnp.where(chosen, by_expert[:, None, :experts], 0.0), axis=2)
    return (
        token_grads,
        prob_grads,
        gate_grad[None],
        up_grad[None],
        down_grad[None],
    )


def solution(mesh):
    dense = mesh.shape["expert"] == 16 and mesh.shape["dp"] == 2
    return jax.shard_map(
        local_dense if dense else local_general,
        mesh=mesh,
        in_specs=(
            P("expert", "dp"),
            P("expert", "dp"),
            P("expert", None),
            P("expert", None),
            P("expert", None, "dp"),
            P("expert", None, "dp"),
            P("expert", None, "dp"),
        ),
        out_specs=(
            P("expert", "dp"),
            P("expert", None),
            P("expert", None, "dp"),
            P("expert", None, "dp"),
            P("expert", None, "dp"),
        ),
        check_vma=False,
    )
```

```python
import functools

import jax
import jax.numpy as jnp
from jax import lax
from jax.experimental import pallas as pl
from jax.experimental.pallas import tpu as pltpu
from jax.sharding import PartitionSpec as P

F32 = jnp.float32
BF16 = jnp.bfloat16
LANES = 128
VMEM = 14 * 1024 * 1024


def contract_last(left_matrix, right_matrix):
    return lax.dot_general(
        left_matrix, right_matrix, (((1,), (1,)), ((), ())), preferred_element_type=jnp.float32
    )


def contract_first(left_matrix, right_matrix):
    return lax.dot_general(
        left_matrix, right_matrix, (((0,), (0,)), ((), ())), preferred_element_type=jnp.float32
    )


def activations(gate_value, up_value, back_value, weights):
    sigmoid_gate = jax.nn.sigmoid(gate_value)
    silu_gate = gate_value * sigmoid_gate
    hidden = (silu_gate * up_value).astype(jnp.bfloat16)
    prob_local = jnp.sum(hidden.astype(jnp.float32) * back_value, axis=1, keepdims=True)
    grad_back = weights * back_value
    grad_gate = (
        grad_back * up_value * sigmoid_gate * (1.0 + gate_value * (1.0 - sigmoid_gate))
    ).astype(jnp.bfloat16)
    grad_up = (grad_back * silu_gate).astype(jnp.bfloat16)
    return (hidden, grad_gate, grad_up, prob_local)


def local_general(tokens, cotangent, router_probs, expert_ids, w_gate, w_up, w_down):
    experts = lax.axis_size("expert")
    local_tokens, top_count = expert_ids.shape
    row_count = local_tokens * top_count
    slot_count = min(local_tokens, max(2, (row_count + experts - 1) // experts * 17 // 16))
    features = tokens.shape[1]
    flat_ids = expert_ids.reshape(-1)
    hit_table = (flat_ids[:, None] == jnp.arange(experts, dtype=jnp.int32)[None, :]).astype(
        jnp.int32
    )
    slot_ranks = jnp.sum(jnp.cumsum(hit_table, axis=0) * hit_table, axis=1) - 1
    slot_places = flat_ids * slot_count + slot_ranks
    slot_table = jnp.full((experts * slot_count,), row_count, jnp.int32)
    slot_table = slot_table.at[slot_places].set(jnp.arange(row_count, dtype=jnp.int32))
    filled = slot_table < row_count
    sources = jnp.minimum(slot_table, row_count - 1)
    owners = sources // top_count
    send_probs = jnp.where(
        filled, router_probs.reshape(-1)[sources], jnp.zeros((), router_probs.dtype)
    )
    send_probs = send_probs.reshape(experts, slot_count)

    def pack_rows(source):
        picked = jnp.where(filled[:, None], source[owners], jnp.zeros((), source.dtype))
        return picked.reshape(experts, slot_count, source.shape[1])

    exchange = functools.partial(
        lax.all_to_all, axis_name="expert", split_axis=0, concat_axis=0, tiled=True
    )
    recv_in, recv_grad, recv_probs = (
        exchange(pack_rows(tokens)),
        exchange(pack_rows(cotangent)),
        exchange(send_probs),
    )
    inputs = recv_in.reshape(experts * slot_count, features)
    grads_in = recv_grad.reshape(experts * slot_count, features)
    weights = recv_probs.reshape(-1).astype(jnp.float32)
    weight_gate = w_gate[0]
    weight_up = w_up[0]
    weight_down = w_down[0]
    gate_part = contract_last(inputs, weight_gate)
    up_part = contract_last(inputs, weight_up)
    back_part = contract_last(grads_in, weight_down)
    gate_value, up_value, back_value = (
        lax.psum(gate_part.astype(jnp.bfloat16), "dp").astype(jnp.float32),
        lax.psum(up_part.astype(jnp.bfloat16), "dp").astype(jnp.float32),
        lax.psum(back_part.astype(jnp.bfloat16), "dp").astype(jnp.float32),
    )
    hidden, grad_gate, grad_up, prob_value = activations(
        gate_value, up_value, back_value, weights[:, None]
    )
    scaled = (weights[:, None] * grads_in).astype(jnp.bfloat16)
    row_term = jnp.dot(grad_gate, weight_gate, preferred_element_type=jnp.float32)
    row_term = (row_term + jnp.dot(grad_up, weight_up, preferred_element_type=jnp.float32)).astype(
        jnp.bfloat16
    )
    gate_grad = contract_first(grad_gate, inputs).astype(jnp.bfloat16)
    up_grad = contract_first(grad_up, inputs).astype(jnp.bfloat16)
    down_grad = contract_first(hidden, scaled).astype(jnp.bfloat16)
    back_terms = exchange(row_term.reshape(experts, slot_count, features))
    back_probs = exchange(prob_value.astype(jnp.bfloat16).reshape(experts, slot_count))
    returned = back_terms.reshape(experts * slot_count, features)[slot_places].astype(jnp.float32)
    token_sum = jnp.sum(returned.reshape(local_tokens, top_count, features), axis=1)
    prob_grads = (
        back_probs.reshape(-1)[slot_places].astype(jnp.float32).reshape(local_tokens, top_count)
    )
    return (
        token_sum.astype(jnp.bfloat16),
        prob_grads,
        gate_grad[None],
        up_grad[None],
        down_grad[None],
    )


def kernel_call(body, operands, outs, scratch=(), name=None):
    return pl.pallas_call(
        body,
        in_specs=[pl.BlockSpec(memory_space=pltpu.VMEM)] * len(operands),
        out_specs=[pl.BlockSpec(memory_space=pltpu.VMEM)] * len(outs),
        out_shape=[jax.ShapeDtypeStruct(shape, dtype) for shape, dtype in outs],
        scratch_shapes=list(scratch),
        compiler_params=pltpu.CompilerParams(vmem_limit_bytes=VMEM),
        cost_estimate=pl.CostEstimate(flops=1000, bytes_accessed=1000, transcendentals=0),
        name=name,
    )(*operands)


def choose_kernel(cuts, first, second, *outs):
    z_index = lax.div(lax.axis_index("expert"), 4)
    edge = (z_index == 0) | (z_index == 3)

    def write(source):
        for (start, end), out in zip(cuts, outs):
            out[...] = source[:, start:end]

    @pl.when(edge)
    def _():
        write(first)

    @pl.when(jnp.logical_not(edge))
    def _():
        write(second)


def choose(first, second, *cuts):
    return kernel_call(
        functools.partial(choose_kernel, cuts),
        (first, second),
        [((first.shape[0], end - start), BF16) for start, end in cuts],
        name="choose",
    )


def tiles(width, tile, body):
    @pl.loop(0, width // tile)
    def _(k):
        body(pl.multiple_of(k * tile, tile))


def pack_kernel(tokens, cotangent, probs, ids, out, ids_here, packed, sems):
    rows, width = tokens.shape
    moves = (
        (ids, ids_here),
        (cotangent, packed.at[:, pl.ds(0, width)]),
        (tokens, packed.at[:, pl.ds(width, width)]),
        (packed, out),
    )
    copies = [
        pltpu.make_async_copy(source, target, sems.at[i])
        for i, (source, target) in enumerate(moves)
    ]
    for copy in copies[:3]:
        copy.start()
    copies[0].wait()
    lane = lax.broadcasted_iota(jnp.int32, (rows, LANES), 1)
    routing = jnp.full((rows, LANES), -1.0, F32)
    weights, choices = probs[...].astype(F32).T, ids_here[...].T
    for k in range(choices.shape[1]):
        routing = jnp.where(lane == choices[:, k : k + 1], weights[:, k : k + 1], routing)
    packed[:, pl.ds(2 * width, LANES)] = routing.astype(BF16)
    copies[1].wait()
    copies[2].wait()
    copies[3].start()
    copies[3].wait()


def pack(tokens, cotangent, probs, ids):
    rows, width = tokens.shape
    columns = 2 * width + LANES
    return pl.pallas_call(
        pack_kernel,
        in_specs=[pl.BlockSpec(memory_space=pl.ANY)] * 2
        + [pl.BlockSpec(memory_space=pltpu.VMEM), pl.BlockSpec(memory_space=pl.ANY)],
        out_specs=pl.BlockSpec(memory_space=pl.ANY),
        out_shape=jax.ShapeDtypeStruct((rows, columns), BF16),
        scratch_shapes=[
            pltpu.VMEM(ids.shape, ids.dtype),
            pltpu.VMEM((rows, columns), BF16),
            pltpu.SemaphoreType.DMA((4,)),
        ],
        compiler_params=pltpu.CompilerParams(vmem_limit_bytes=60 * 1024 * 1024),
        cost_estimate=pl.CostEstimate(flops=1000, bytes_accessed=1000, transcendentals=0),
        name="pack",
    )(tokens, cotangent, probs, ids)


def front_kernel(slots, layout, joined, *refs):
    sources = refs[: sum(layout)]
    w_gate, w_up, w_down = refs[len(sources) : len(sources) + 3]
    *outs, acc, picks = refs[len(sources) + 3 :]
    units, width = w_gate.shape
    block = sources[0].shape[0]
    pairs = len(layout) // 2
    rows = picks.shape[1]
    tile = 1024
    expert = lax.axis_index("expert")

    blocks, start = [], 0
    for size in layout:
        here = sources[start : start + size]
        blocks.append((here[0], here[-1], width if size == 1 else 0))
        start = start + size

    lane = lax.broadcasted_iota(jnp.int32, (block, LANES), 1)
    tri = (
        lax.broadcasted_iota(jnp.int32, (block, block), 1)
        <= lax.broadcasted_iota(jnp.int32, (block, block), 0)
    ).astype(BF16)
    for p in range(pairs):
        spread, weights = outs[4 * p + 2], outs[4 * p + 3]
        total = jnp.zeros((rows, LANES), F32)
        for b, (_, source, offset) in enumerate(blocks[2 * p : 2 * p + 2]):
            routing = source[:, pl.ds(offset + width, LANES)].astype(F32)
            prob = jnp.sum(jnp.where(lane == expert, routing, 0.0), axis=1, keepdims=True)
            chosen = jnp.broadcast_to(prob >= 0.0, (block, LANES))
            rank = jnp.dot(tri, chosen.astype(BF16), preferred_element_type=F32)
            slot = jnp.where(chosen, rank + (slots * b - 1.0), -1.0)
            spread[pl.ds(b * block, block), :] = (
                lax.broadcasted_iota(jnp.int32, (block, rows), 1)
                == slot[:, :1].astype(jnp.int32)
            ).astype(BF16)
            slot_row = slot.T[:1, :].astype(jnp.int32)
            picked = (lax.broadcasted_iota(jnp.int32, (rows, block), 0) == slot_row).astype(BF16)
            picks[p, :, pl.ds(b * block, block)] = picked
            prob = jnp.broadcast_to(jnp.maximum(prob, 0.0), (block, LANES)).astype(BF16)
            total = total + jnp.dot(picked, prob, preferred_element_type=F32)
        weights[...] = total
    acc[...] = jnp.zeros(acc.shape, F32)

    def step(start):
        here = pl.ds(start, tile)
        rows_in, grads_in = [], []
        for p in range(pairs):
            inputs, scaled, _, weights = outs[4 * p : 4 * p + 4]
            (first_c, first_t, first_at), (second_c, second_t, second_at) = blocks[2 * p : 2 * p + 2]
            stacked = jnp.concatenate(
                [
                    first_t[:, pl.ds(first_at + start, tile)],
                    second_t[:, pl.ds(second_at + start, tile)],
                ],
                axis=0,
            )
            picked = jnp.dot(picks[p], stacked, preferred_element_type=F32).astype(BF16)
            inputs[:, here] = picked
            rows_in.append(picked)
            stacked = jnp.concatenate([first_c[:, here], second_c[:, here]], axis=0)
            picked = jnp.dot(picks[p], stacked, preferred_element_type=F32)
            scaled[:, here] = (weights[:, :1] * picked).astype(BF16)
            grads_in.append(picked.astype(BF16))
        rows_in = jnp.concatenate(rows_in, axis=0)
        acc[:, :units] += contract_last(rows_in, w_gate[:, here])
        acc[:, units : 2 * units] += contract_last(rows_in, w_up[:, here])
        acc[:, 2 * units :] += contract_last(jnp.concatenate(grads_in, axis=0), w_down[:, here])

    tiles(width, tile, step)
    if joined:
        outs[-1][...] = jnp.concatenate(
            [acc[p * rows : p * rows + 2 * slots] for p in range(pairs)], axis=0
        ).astype(BF16)
    else:
        for p in range(pairs):
            outs[4 * pairs + p][...] = acc[p * rows : p * rows + 2 * slots].astype(BF16)


def front(blocks, w_gate, w_up, w_down, slots, joined):
    blocks = [b if isinstance(b, tuple) else (b,) for b in blocks]
    layout = [len(b) for b in blocks]
    sources = [array for b in blocks for array in b]
    block = sources[0].shape[0]
    units, width = w_gate.shape
    pairs = len(blocks) // 2
    rows = -(-2 * slots // 16) * 16
    results = kernel_call(
        functools.partial(front_kernel, slots, layout, joined),
        (*sources, w_gate, w_up, w_down),
        [
            ((rows, width), BF16),
            ((rows, width), BF16),
            ((2 * block, rows), BF16),
            ((rows, LANES), F32),
        ]
        * pairs
        + [((2 * slots * (pairs if joined else 1), 3 * units), BF16)] * (1 if joined else pairs),
        scratch=[
            pltpu.VMEM((pairs * rows, 3 * units), F32),
            pltpu.VMEM((pairs, rows, 2 * block), BF16),
        ],
        name="front",
    )
    names = ("inputs", "scaled", "spread", "weights")
    states = [dict(zip(names, results[4 * p : 4 * p + 4])) for p in range(pairs)]
    return states, results[4 * pairs :]


def back_kernel(pairs, own, peer, *refs):
    weights, spreads = refs[:pairs], refs[pairs : 2 * pairs]
    w_gate, w_up, hidden, grad_gate, grad_up, *outs = refs[2 * pairs :]
    units, width = w_gate.shape
    filled = own.shape[0] // pairs
    tokens, rows = spreads[0].shape
    tile = 1024
    expert = lax.axis_index("expert")

    def place(term, columns):
        for p in range(pairs):
            here = term[p * rows : (p + 1) * rows]
            placed = jnp.dot(spreads[p][...], here, preferred_element_type=F32).astype(BF16)
            outs[2 * p][:, columns] = placed[: tokens // 2]
            outs[2 * p + 1][:, columns] = placed[tokens // 2 :]

    def value(i):
        columns = pl.ds(i * units, units)
        total = own[:, columns].astype(F32) + peer[:, columns].astype(F32)
        if rows == filled:
            return total
        pad = jnp.zeros((rows - filled, units), F32)
        pieces = [total[p * filled : (p + 1) * filled] for p in range(pairs)]
        return jnp.concatenate([piece for each in pieces for piece in (each, pad)], axis=0)

    scales = jnp.concatenate([weight[:, :1] for weight in weights], axis=0)
    h, gg, gu, prob = activations(value(0), value(1), value(2), scales)
    hidden[...] = h
    grad_gate[...] = gg
    grad_up[...] = gu
    lane = lax.broadcasted_iota(jnp.int32, (pairs * rows, LANES), 1)
    place(jnp.where(lane == expert, prob, 0.0).astype(BF16), pl.ds(width, LANES))

    def step(start):
        columns = pl.ds(start, tile)
        term = jnp.dot(grad_gate[...], w_gate[:, columns], preferred_element_type=F32)
        term = term + jnp.dot(grad_up[...], w_up[:, columns], preferred_element_type=F32)
        place(term.astype(BF16), columns)

    tiles(width, tile, step)


def back(states, own, peer, w_gate, w_up):
    units, width = w_gate.shape
    pairs = len(states)
    tokens, rows = states[0]["spread"].shape
    half = (tokens // 2, width + LANES)
    results = kernel_call(
        functools.partial(back_kernel, pairs),
        (
            own,
            peer,
            *[state["weights"] for state in states],
            *[state["spread"] for state in states],
            w_gate,
            w_up,
        ),
        [((pairs * rows, units), BF16)] * 3 + [(half, BF16)] * (2 * pairs),
        name="back",
    )
    return results[:3], [results[3 + 2 * p : 5 + 2 * p] for p in range(pairs)]


def outer_kernel(count, *refs):
    *terms, out, turned = refs
    lefts, rights = terms[:count], terms[count:]

    @pl.when(pl.program_id(0) == 0)
    def _():
        turned[...] = jnp.concatenate([left[...] for left in lefts], axis=0).T

    right = jnp.concatenate([right[...] for right in rights], axis=0)
    out[...] = jnp.dot(turned[...], right, preferred_element_type=F32).astype(BF16)


def outer(lefts, rights):
    units, width = lefts[0].shape[1], rights[0].shape[1]
    rows = sum(left.shape[0] for left in lefts)
    tile = 512
    return pl.pallas_call(
        functools.partial(outer_kernel, len(lefts)),
        grid=(width // tile,),
        in_specs=[pl.BlockSpec(left.shape, lambda k: (0, 0)) for left in lefts]
        + [pl.BlockSpec((right.shape[0], tile), lambda k: (0, k)) for right in rights],
        out_specs=pl.BlockSpec((units, tile), lambda k: (0, k)),
        out_shape=jax.ShapeDtypeStruct((units, width), BF16),
        scratch_shapes=[pltpu.VMEM((units, rows), BF16)],
        compiler_params=pltpu.CompilerParams(vmem_limit_bytes=VMEM),
        cost_estimate=pl.CostEstimate(flops=1000, bytes_accessed=1000, transcendentals=0),
        name="outer",
    )(*lefts, *rights)


def add_kernel(*refs):
    *terms, out = refs
    total = terms[0][...].astype(F32)
    for term in terms[1:]:
        total = total + term[...].astype(F32)
    out[...] = total.astype(BF16)


def add(*terms):
    return kernel_call(add_kernel, terms, [(terms[0].shape, BF16)], name="add")[0]


def finish_kernel(*refs):
    *terms, tokens_out, probs_out = refs
    total = terms[0][...].astype(F32)
    for term in terms[1:]:
        total = total + term[...].astype(F32)
    width = tokens_out.shape[1]
    tokens_out[...] = total[:, :width].astype(BF16)
    probs_out[...] = total[:, width:]


def finish(*terms):
    block, columns = terms[0].shape
    outs = [((block, columns - LANES), BF16), ((block, LANES), F32)]
    return kernel_call(finish_kernel, terms, outs, name="finish")


def meet(*values):
    return lax.optimization_barrier(values)


def local_dense(tokens, cotangent, router_probs, expert_ids, w_gate, w_up, w_down):
    experts = lax.axis_size("expert")
    block, top_count = expert_ids.shape
    row_count = block * top_count
    slots = min(block, max(2, (row_count + experts - 1) // experts * 17 // 16))
    weight_gate, weight_up, weight_down = w_gate[0], w_up[0], w_down[0]

    def swap(value, bits, part=(0, 1, 2, 3)):
        pairs = [(i, i ^ bits) for i in range(experts) if i // 4 in part]
        return lax.ppermute(value, "expert", pairs)

    core = functools.partial(swap, bits=1)
    across = functools.partial(swap, bits=2)
    outer_z = functools.partial(swap, bits=4)
    inner_z = functools.partial(swap, bits=12, part=(1, 2))
    to_edge = functools.partial(swap, bits=4, part=(1, 2))

    rights, lefts = [], []

    def forward(*blocks, joined=False):
        return front(blocks, weight_gate, weight_up, weight_down, slots, joined)

    def exchange(part):
        return lax.ppermute(part, "dp", [(0, 1), (1, 0)])

    def backward(states, own, peer):
        left, sums = back(states, own, peer, weight_gate, weight_up)
        rights.extend((state["inputs"], state["scaled"]) for state in states)
        lefts.append(left)
        return sums, left[0]

    features = tokens.shape[1]
    all_columns = 2 * features + LANES

    p0 = pack(tokens, cotangent, router_probs.T, expert_ids.T)
    q0 = core(p0)
    p1, a0, m0 = across(p0), outer_z(p0), inner_z(p0)
    (state0,), (part0,) = forward(p0, q0)

    p1, a0, m0, part0 = meet(p1, a0, m0, part0)
    a1, b0e, c0m = across(a0), to_edge(m0), inner_z(a0)
    states1, (part1,) = forward(p1, core(p1), a0, core(a0), joined=True)
    y1 = exchange(part1)

    (b0,) = choose(b0e, m0, (0, all_columns))
    a1, b0, c0m, _ = meet(a1, b0, c0m, part1)
    b1, c0e = across(b0), to_edge(c0m)
    (state_a1, state_b0), (part_a1, part_b0) = forward(a1, core(a1), b0, core(b0))

    y1, part_a1 = meet(y1, part_a1)
    ya1 = exchange(part_a1)
    ((keep1, send1), (keep_a0, send_a0)), done = backward(states1, part1, y1)
    k1, ka0 = core(send1), core(send_a0)

    columns = (0, all_columns), (0, features), (features, all_columns)
    c0, c0c, c0t = choose(c0e, c0m, *columns)
    b1, c0, c0c, c0t, ya1, part_b0, k1, ka0 = meet(
        b1, c0, c0c, c0t, ya1, part_b0, k1, ka0
    )
    yb0 = exchange(part_b0)
    c1c, c1t = across(c0c), across(c0t)
    (state_b1, state_c0), (part_b1, part_c0) = forward(b1, core(b1), c0, core(c0))
    ((keep_a1, send_a1),), done = backward((state_a1,), part_a1, ya1)

    yb0, part_b1, send_a1 = meet(yb0, part_b1, send_a1)
    yb1 = exchange(part_b1)
    ka1 = core(send_a1)
    qc1 = core(c1c), core(c1t)
    ((keep_b0, send_b0),), done = backward((state_b0,), part_b0, yb0)
    kb0 = core(send_b0)

    part_c0, ka1, yb1, kb0, *qc1 = meet(part_c0, ka1, yb1, kb0, *qc1)
    yc0 = exchange(part_c0)
    ra = across(add(keep_a1, ka1))
    sum1 = add(keep1, k1)
    sumb0 = add(keep_b0, kb0)
    ((keep_b1, send_b1),), done = backward((state_b1,), part_b1, yb1)
    kb1 = core(send_b1)
    (state_c1,), (part_c1,) = forward((c1c, c1t), tuple(qc1))

    suma = add(keep_a0, ka0, ra)
    part_c1, yc0, suma, sum1, sumb0, keep_b1 = meet(part_c1, yc0, suma, sum1, sumb0, keep_b1)
    yc1 = exchange(part_c1)
    rb = across(add(keep_b1, kb1))
    from_a = outer_z(suma)
    ((keep_c0, send_c0),), done = backward((state_c0,), part_c0, yc0)
    kc0 = core(send_c0)

    yc1, rb, from_a, part0, keep_c0 = meet(yc1, rb, from_a, part0, keep_c0)
    y0 = exchange(part0)
    ((keep_c1, send_c1),), done = backward((state_c1,), part_c1, yc1)
    kc1 = core(send_c1)
    sumc0 = add(keep_c0, kc0)
    sumb = add(sumb0, rb)
    b_edge, b_middle = swap(sumb, 8, (0, 3)), swap(sumb, 12, (1, 2))

    sumc1 = add(keep_c1, kc1)
    rc = across(sumc1)
    rc, sum1 = meet(rc, sum1)
    sumc = add(sumc0, rc)
    c_edge = outer_z(sumc, part=(0, 3))
    r0 = across(sum1)
    y0, _ = meet(y0, sumc)
    ((keep0, send0),), done = backward((state0,), part0, y0)
    k0 = core(send0)

    inputs, scaled = zip(*rights)
    hidden, grad_gate, grad_up = zip(*lefts)
    gate_grad = outer(grad_gate, inputs)

    c_edge, b_edge, b_middle, _ = meet(c_edge, b_edge, b_middle, gate_grad)
    sumc = add(sumc, c_edge)
    sumc, k0 = meet(sumc, k0)
    far = swap(sumc, 8, (1, 2))
    grad_up, _ = meet(grad_up, sumc)
    up_grad = outer(grad_up, inputs)
    hidden, _ = meet(hidden, up_grad)
    down_grad = outer(hidden, scaled)
    r0, _ = meet(r0, down_grad)
    near = add(keep0, k0, r0, from_a, b_edge, b_middle)
    far, near = meet(far, near)
    token_grads, by_expert = finish(near, far)
    chosen = expert_ids[:, :, None] == jnp.arange(experts, dtype=jnp.int32)[None, None, :]
    prob_grads = jnp.sum(jnp.where(chosen, by_expert[:, None, :experts], 0.0), axis=2)
    return (
        token_grads,
        prob_grads,
        gate_grad[None],
        up_grad[None],
        down_grad[None],
    )


def solution(mesh):
    dense = mesh.shape["expert"] == 16 and mesh.shape["dp"] == 2
    return jax.shard_map(
        local_dense if dense else local_general,
        mesh=mesh,
        in_specs=(
            P("expert", "dp"),
            P("expert", "dp"),
            P("expert", None),
            P("expert", None),
            P("expert", None, "dp"),
            P("expert", None, "dp"),
            P("expert", None, "dp"),
        ),
        out_specs=(
            P("expert", "dp"),
            P("expert", None),
            P("expert", None, "dp"),
            P("expert", None, "dp"),
            P("expert", None, "dp"),
        ),
        check_vma=False,
    )
```

```python
import functools

import jax
import jax.numpy as jnp
from jax import lax
from jax.experimental import pallas as pl
from jax.experimental.pallas import tpu as pltpu
from jax.sharding import PartitionSpec as P

F32 = jnp.float32
BF16 = jnp.bfloat16
LANES = 128
VMEM = 14 * 1024 * 1024


def contract_last(left_matrix, right_matrix):
    return lax.dot_general(
        left_matrix, right_matrix, (((1,), (1,)), ((), ())), preferred_element_type=jnp.float32
    )


def contract_first(left_matrix, right_matrix):
    return lax.dot_general(
        left_matrix, right_matrix, (((0,), (0,)), ((), ())), preferred_element_type=jnp.float32
    )


def activations(gate_value, up_value, back_value, weights):
    sigmoid_gate = jax.nn.sigmoid(gate_value)
    silu_gate = gate_value * sigmoid_gate
    hidden = (silu_gate * up_value).astype(jnp.bfloat16)
    prob_local = jnp.sum(hidden.astype(jnp.float32) * back_value, axis=1, keepdims=True)
    grad_back = weights * back_value
    grad_gate = (
        grad_back * up_value * sigmoid_gate * (1.0 + gate_value * (1.0 - sigmoid_gate))
    ).astype(jnp.bfloat16)
    grad_up = (grad_back * silu_gate).astype(jnp.bfloat16)
    return (hidden, grad_gate, grad_up, prob_local)


def local_general(tokens, cotangent, router_probs, expert_ids, w_gate, w_up, w_down):
    experts = lax.axis_size("expert")
    local_tokens, top_count = expert_ids.shape
    row_count = local_tokens * top_count
    slot_count = min(local_tokens, max(2, (row_count + experts - 1) // experts * 17 // 16))
    features = tokens.shape[1]
    flat_ids = expert_ids.reshape(-1)
    hit_table = (flat_ids[:, None] == jnp.arange(experts, dtype=jnp.int32)[None, :]).astype(
        jnp.int32
    )
    slot_ranks = jnp.sum(jnp.cumsum(hit_table, axis=0) * hit_table, axis=1) - 1
    slot_places = flat_ids * slot_count + slot_ranks
    slot_table = jnp.full((experts * slot_count,), row_count, jnp.int32)
    slot_table = slot_table.at[slot_places].set(jnp.arange(row_count, dtype=jnp.int32))
    filled = slot_table < row_count
    sources = jnp.minimum(slot_table, row_count - 1)
    owners = sources // top_count
    send_probs = jnp.where(
        filled, router_probs.reshape(-1)[sources], jnp.zeros((), router_probs.dtype)
    )
    send_probs = send_probs.reshape(experts, slot_count)

    def pack_rows(source):
        picked = jnp.where(filled[:, None], source[owners], jnp.zeros((), source.dtype))
        return picked.reshape(experts, slot_count, source.shape[1])

    exchange = functools.partial(
        lax.all_to_all, axis_name="expert", split_axis=0, concat_axis=0, tiled=True
    )
    recv_in, recv_grad, recv_probs = (
        exchange(pack_rows(tokens)),
        exchange(pack_rows(cotangent)),
        exchange(send_probs),
    )
    inputs = recv_in.reshape(experts * slot_count, features)
    grads_in = recv_grad.reshape(experts * slot_count, features)
    weights = recv_probs.reshape(-1).astype(jnp.float32)
    weight_gate = w_gate[0]
    weight_up = w_up[0]
    weight_down = w_down[0]
    gate_part = contract_last(inputs, weight_gate)
    up_part = contract_last(inputs, weight_up)
    back_part = contract_last(grads_in, weight_down)
    gate_value, up_value, back_value = (
        lax.psum(gate_part.astype(jnp.bfloat16), "dp").astype(jnp.float32),
        lax.psum(up_part.astype(jnp.bfloat16), "dp").astype(jnp.float32),
        lax.psum(back_part.astype(jnp.bfloat16), "dp").astype(jnp.float32),
    )
    hidden, grad_gate, grad_up, prob_value = activations(
        gate_value, up_value, back_value, weights[:, None]
    )
    scaled = (weights[:, None] * grads_in).astype(jnp.bfloat16)
    row_term = jnp.dot(grad_gate, weight_gate, preferred_element_type=jnp.float32)
    row_term = (row_term + jnp.dot(grad_up, weight_up, preferred_element_type=jnp.float32)).astype(
        jnp.bfloat16
    )
    gate_grad = contract_first(grad_gate, inputs).astype(jnp.bfloat16)
    up_grad = contract_first(grad_up, inputs).astype(jnp.bfloat16)
    down_grad = contract_first(hidden, scaled).astype(jnp.bfloat16)
    back_terms = exchange(row_term.reshape(experts, slot_count, features))
    back_probs = exchange(prob_value.astype(jnp.bfloat16).reshape(experts, slot_count))
    returned = back_terms.reshape(experts * slot_count, features)[slot_places].astype(jnp.float32)
    token_sum = jnp.sum(returned.reshape(local_tokens, top_count, features), axis=1)
    prob_grads = (
        back_probs.reshape(-1)[slot_places].astype(jnp.float32).reshape(local_tokens, top_count)
    )
    return (
        token_sum.astype(jnp.bfloat16),
        prob_grads,
        gate_grad[None],
        up_grad[None],
        down_grad[None],
    )


def kernel_call(body, operands, outs, scratch=(), name=None):
    return pl.pallas_call(
        body,
        in_specs=[pl.BlockSpec(memory_space=pltpu.VMEM)] * len(operands),
        out_specs=[pl.BlockSpec(memory_space=pltpu.VMEM)] * len(outs),
        out_shape=[jax.ShapeDtypeStruct(shape, dtype) for shape, dtype in outs],
        scratch_shapes=list(scratch),
        compiler_params=pltpu.CompilerParams(vmem_limit_bytes=VMEM),
        cost_estimate=pl.CostEstimate(flops=1000, bytes_accessed=1000, transcendentals=0),
        name=name,
    )(*operands)


def choose_kernel(cuts, first, second, *outs):
    z_index = lax.div(lax.axis_index("expert"), 4)
    edge = (z_index == 0) | (z_index == 3)

    def write(source):
        for (start, end), out in zip(cuts, outs):
            out[...] = source[:, start:end]

    @pl.when(edge)
    def _():
        write(first)

    @pl.when(jnp.logical_not(edge))
    def _():
        write(second)


def choose(first, second, *cuts):
    return kernel_call(
        functools.partial(choose_kernel, cuts),
        (first, second),
        [((first.shape[0], end - start), BF16) for start, end in cuts],
        name="choose",
    )


def tiles(width, tile, body):
    @pl.loop(0, width // tile)
    def _(k):
        body(pl.multiple_of(k * tile, tile))


def pack_kernel(tokens, cotangent, probs, ids, out, ids_here, packed, sems):
    rows, width = tokens.shape
    moves = (
        (ids, ids_here),
        (cotangent, packed.at[:, pl.ds(0, width)]),
        (tokens, packed.at[:, pl.ds(width, width)]),
        (packed, out),
    )
    copies = [
        pltpu.make_async_copy(source, target, sems.at[i])
        for i, (source, target) in enumerate(moves)
    ]
    for copy in copies[:3]:
        copy.start()
    copies[0].wait()
    lane = lax.broadcasted_iota(jnp.int32, (rows, LANES), 1)
    routing = jnp.full((rows, LANES), -1.0, F32)
    weights, choices = probs[...].astype(F32).T, ids_here[...].T
    for k in range(choices.shape[1]):
        routing = jnp.where(lane == choices[:, k : k + 1], weights[:, k : k + 1], routing)
    packed[:, pl.ds(2 * width, LANES)] = routing.astype(BF16)
    copies[1].wait()
    copies[2].wait()
    copies[3].start()
    copies[3].wait()


def pack(tokens, cotangent, probs, ids):
    rows, width = tokens.shape
    columns = 2 * width + LANES
    return pl.pallas_call(
        pack_kernel,
        in_specs=[pl.BlockSpec(memory_space=pl.ANY)] * 2
        + [pl.BlockSpec(memory_space=pltpu.VMEM), pl.BlockSpec(memory_space=pl.ANY)],
        out_specs=pl.BlockSpec(memory_space=pl.ANY),
        out_shape=jax.ShapeDtypeStruct((rows, columns), BF16),
        scratch_shapes=[
            pltpu.VMEM(ids.shape, ids.dtype),
            pltpu.VMEM((rows, columns), BF16),
            pltpu.SemaphoreType.DMA((4,)),
        ],
        compiler_params=pltpu.CompilerParams(vmem_limit_bytes=60 * 1024 * 1024),
        cost_estimate=pl.CostEstimate(flops=1000, bytes_accessed=1000, transcendentals=0),
        name="pack",
    )(tokens, cotangent, probs, ids)


def front_kernel(slots, layout, joined, *refs):
    sources = refs[: sum(layout)]
    w_gate, w_up, w_down = refs[len(sources) : len(sources) + 3]
    *outs, acc, picks = refs[len(sources) + 3 :]
    units, width = w_gate.shape
    block = sources[0].shape[0]
    pairs = len(layout) // 2
    rows = picks.shape[1]
    tile = 1024
    expert = lax.axis_index("expert")

    blocks, start = [], 0
    for size in layout:
        here = sources[start : start + size]
        blocks.append((here[0], here[-1], width if size == 1 else 0))
        start = start + size

    lane = lax.broadcasted_iota(jnp.int32, (block, LANES), 1)
    tri = (
        lax.broadcasted_iota(jnp.int32, (block, block), 1)
        <= lax.broadcasted_iota(jnp.int32, (block, block), 0)
    ).astype(BF16)
    for p in range(pairs):
        spread, weights = outs[4 * p + 2], outs[4 * p + 3]
        total = jnp.zeros((rows, LANES), F32)
        for b, (_, source, offset) in enumerate(blocks[2 * p : 2 * p + 2]):
            routing = source[:, pl.ds(offset + width, LANES)].astype(F32)
            prob = jnp.sum(jnp.where(lane == expert, routing, 0.0), axis=1, keepdims=True)
            chosen = jnp.broadcast_to(prob >= 0.0, (block, LANES))
            rank = jnp.dot(tri, chosen.astype(BF16), preferred_element_type=F32)
            slot = jnp.where(chosen, rank + (slots * b - 1.0), -1.0)
            spread[pl.ds(b * block, block), :] = (
                lax.broadcasted_iota(jnp.int32, (block, rows), 1)
                == slot[:, :1].astype(jnp.int32)
            ).astype(BF16)
            slot_row = slot.T[:1, :].astype(jnp.int32)
            picked = (lax.broadcasted_iota(jnp.int32, (rows, block), 0) == slot_row).astype(BF16)
            picks[p, :, pl.ds(b * block, block)] = picked
            prob = jnp.broadcast_to(jnp.maximum(prob, 0.0), (block, LANES)).astype(BF16)
            total = total + jnp.dot(picked, prob, preferred_element_type=F32)
        weights[...] = total
    acc[...] = jnp.zeros(acc.shape, F32)

    def step(start):
        here = pl.ds(start, tile)
        rows_in, grads_in = [], []
        for p in range(pairs):
            inputs, scaled, _, weights = outs[4 * p : 4 * p + 4]
            (first_c, first_t, first_at), (second_c, second_t, second_at) = blocks[2 * p : 2 * p + 2]
            stacked = jnp.concatenate(
                [
                    first_t[:, pl.ds(first_at + start, tile)],
                    second_t[:, pl.ds(second_at + start, tile)],
                ],
                axis=0,
            )
            picked = jnp.dot(picks[p], stacked, preferred_element_type=F32).astype(BF16)
            inputs[:, here] = picked
            rows_in.append(picked)
            stacked = jnp.concatenate([first_c[:, here], second_c[:, here]], axis=0)
            picked = jnp.dot(picks[p], stacked, preferred_element_type=F32)
            scaled[:, here] = (weights[:, :1] * picked).astype(BF16)
            grads_in.append(picked.astype(BF16))
        rows_in = jnp.concatenate(rows_in, axis=0)
        acc[:, :units] += contract_last(rows_in, w_gate[:, here])
        acc[:, units : 2 * units] += contract_last(rows_in, w_up[:, here])
        acc[:, 2 * units :] += contract_last(jnp.concatenate(grads_in, axis=0), w_down[:, here])

    tiles(width, tile, step)
    if joined:
        outs[-1][...] = jnp.concatenate(
            [acc[p * rows : p * rows + 2 * slots] for p in range(pairs)], axis=0
        ).astype(BF16)
    else:
        for p in range(pairs):
            outs[4 * pairs + p][...] = acc[p * rows : p * rows + 2 * slots].astype(BF16)


def front(blocks, w_gate, w_up, w_down, slots, joined):
    blocks = [b if isinstance(b, tuple) else (b,) for b in blocks]
    layout = [len(b) for b in blocks]
    sources = [array for b in blocks for array in b]
    block = sources[0].shape[0]
    units, width = w_gate.shape
    pairs = len(blocks) // 2
    rows = -(-2 * slots // 16) * 16
    results = kernel_call(
        functools.partial(front_kernel, slots, layout, joined),
        (*sources, w_gate, w_up, w_down),
        [
            ((rows, width), BF16),
            ((rows, width), BF16),
            ((2 * block, rows), BF16),
            ((rows, LANES), F32),
        ]
        * pairs
        + [((2 * slots * (pairs if joined else 1), 3 * units), BF16)] * (1 if joined else pairs),
        scratch=[
            pltpu.VMEM((pairs * rows, 3 * units), F32),
            pltpu.VMEM((pairs, rows, 2 * block), BF16),
        ],
        name="front",
    )
    names = ("inputs", "scaled", "spread", "weights")
    states = [dict(zip(names, results[4 * p : 4 * p + 4])) for p in range(pairs)]
    return states, results[4 * pairs :]


def back_kernel(pairs, own, peer, *refs):
    weights, spreads = refs[:pairs], refs[pairs : 2 * pairs]
    w_gate, w_up, hidden, grad_gate, grad_up, *outs = refs[2 * pairs :]
    units, width = w_gate.shape
    filled = own.shape[0] // pairs
    tokens, rows = spreads[0].shape
    tile = 1024
    expert = lax.axis_index("expert")

    def place(term, columns):
        for p in range(pairs):
            here = term[p * rows : (p + 1) * rows]
            placed = jnp.dot(spreads[p][...], here, preferred_element_type=F32).astype(BF16)
            outs[2 * p][:, columns] = placed[: tokens // 2]
            outs[2 * p + 1][:, columns] = placed[tokens // 2 :]

    def value(i):
        columns = pl.ds(i * units, units)
        total = own[:, columns].astype(F32) + peer[:, columns].astype(F32)
        if rows == filled:
            return total
        pad = jnp.zeros((rows - filled, units), F32)
        pieces = [total[p * filled : (p + 1) * filled] for p in range(pairs)]
        return jnp.concatenate([piece for each in pieces for piece in (each, pad)], axis=0)

    scales = jnp.concatenate([weight[:, :1] for weight in weights], axis=0)
    h, gg, gu, prob = activations(value(0), value(1), value(2), scales)
    hidden[...] = h
    grad_gate[...] = gg
    grad_up[...] = gu
    lane = lax.broadcasted_iota(jnp.int32, (pairs * rows, LANES), 1)
    place(jnp.where(lane == expert, prob, 0.0).astype(BF16), pl.ds(width, LANES))

    def step(start):
        columns = pl.ds(start, tile)
        term = jnp.dot(grad_gate[...], w_gate[:, columns], preferred_element_type=F32)
        term = term + jnp.dot(grad_up[...], w_up[:, columns], preferred_element_type=F32)
        place(term.astype(BF16), columns)

    tiles(width, tile, step)


def back(states, own, peer, w_gate, w_up):
    units, width = w_gate.shape
    pairs = len(states)
    tokens, rows = states[0]["spread"].shape
    half = (tokens // 2, width + LANES)
    results = kernel_call(
        functools.partial(back_kernel, pairs),
        (
            own,
            peer,
            *[state["weights"] for state in states],
            *[state["spread"] for state in states],
            w_gate,
            w_up,
        ),
        [((pairs * rows, units), BF16)] * 3 + [(half, BF16)] * (2 * pairs),
        name="back",
    )
    return results[:3], [results[3 + 2 * p : 5 + 2 * p] for p in range(pairs)]


def outer_kernel(count, *refs):
    *terms, out, turned = refs
    lefts, rights = terms[:count], terms[count:]

    @pl.when(pl.program_id(0) == 0)
    def _():
        turned[...] = jnp.concatenate([left[...] for left in lefts], axis=0).T

    right = jnp.concatenate([right[...] for right in rights], axis=0)
    out[...] = jnp.dot(turned[...], right, preferred_element_type=F32).astype(BF16)


def outer(lefts, rights):
    units, width = lefts[0].shape[1], rights[0].shape[1]
    rows = sum(left.shape[0] for left in lefts)
    tile = 512
    return pl.pallas_call(
        functools.partial(outer_kernel, len(lefts)),
        grid=(width // tile,),
        in_specs=[pl.BlockSpec(left.shape, lambda k: (0, 0)) for left in lefts]
        + [pl.BlockSpec((right.shape[0], tile), lambda k: (0, k)) for right in rights],
        out_specs=pl.BlockSpec((units, tile), lambda k: (0, k)),
        out_shape=jax.ShapeDtypeStruct((units, width), BF16),
        scratch_shapes=[pltpu.VMEM((units, rows), BF16)],
        compiler_params=pltpu.CompilerParams(vmem_limit_bytes=VMEM),
        cost_estimate=pl.CostEstimate(flops=1000, bytes_accessed=1000, transcendentals=0),
        name="outer",
    )(*lefts, *rights)


def add_kernel(*refs):
    *terms, out = refs
    total = terms[0][...].astype(F32)
    for term in terms[1:]:
        total = total + term[...].astype(F32)
    out[...] = total.astype(BF16)


def add(*terms):
    return kernel_call(add_kernel, terms, [(terms[0].shape, BF16)], name="add")[0]


def finish_kernel(*refs):
    *terms, tokens_out, probs_out = refs
    total = terms[0][...].astype(F32)
    for term in terms[1:]:
        total = total + term[...].astype(F32)
    width = tokens_out.shape[1]
    tokens_out[...] = total[:, :width].astype(BF16)
    probs_out[...] = total[:, width:]


def finish(*terms):
    block, columns = terms[0].shape
    outs = [((block, columns - LANES), BF16), ((block, LANES), F32)]
    return kernel_call(finish_kernel, terms, outs, name="finish")


def meet(*values):
    return lax.optimization_barrier(values)


def local_dense(tokens, cotangent, router_probs, expert_ids, w_gate, w_up, w_down):
    experts = lax.axis_size("expert")
    block, top_count = expert_ids.shape
    row_count = block * top_count
    slots = min(block, max(2, (row_count + experts - 1) // experts * 17 // 16))
    weight_gate, weight_up, weight_down = w_gate[0], w_up[0], w_down[0]

    def swap(value, bits, part=(0, 1, 2, 3)):
        pairs = [(i, i ^ bits) for i in range(experts) if i // 4 in part]
        return lax.ppermute(value, "expert", pairs)

    core = functools.partial(swap, bits=1)
    across = functools.partial(swap, bits=2)
    outer_z = functools.partial(swap, bits=4)
    inner_z = functools.partial(swap, bits=12, part=(1, 2))

    rights, lefts = [], []

    def forward(*blocks, joined=False):
        return front(blocks, weight_gate, weight_up, weight_down, slots, joined)

    def exchange(part):
        return lax.ppermute(part, "dp", [(0, 1), (1, 0)])

    def backward(states, own, peer):
        left, sums = back(states, own, peer, weight_gate, weight_up)
        rights.extend((state["inputs"], state["scaled"]) for state in states)
        lefts.append(left)
        return sums, left[0]

    features = tokens.shape[1]
    all_columns = 2 * features + LANES

    p0 = pack(tokens, cotangent, router_probs.T, expert_ids.T)
    q0 = core(p0)
    p1, a0, m0 = across(p0), outer_z(p0), inner_z(p0)
    (state0,), (part0,) = forward(p0, q0)

    p1, a0, m0, part0 = meet(p1, a0, m0, part0)
    a1, b0e, c0m = across(a0), outer_z(m0), inner_z(a0)
    states1, (part1,) = forward(p1, core(p1), a0, core(a0), joined=True)
    y1 = exchange(part1)

    (b0,) = choose(b0e, m0, (0, all_columns))
    a1, b0, c0m, _ = meet(a1, b0, c0m, part1)
    b1, c0e = across(b0), outer_z(c0m)
    (state_a1, state_b0), (part_a1, part_b0) = forward(a1, core(a1), b0, core(b0))

    y1, part_a1 = meet(y1, part_a1)
    ya1 = exchange(part_a1)
    ((keep1, send1), (keep_a0, send_a0)), done = backward(states1, part1, y1)
    k1, ka0 = core(send1), core(send_a0)

    columns = (0, all_columns), (0, features), (features, all_columns)
    c0, c0c, c0t = choose(c0e, c0m, *columns)
    b1, c0, c0c, c0t, ya1, part_b0, k1, ka0 = meet(
        b1, c0, c0c, c0t, ya1, part_b0, k1, ka0
    )
    yb0 = exchange(part_b0)
    c1c, c1t = across(c0c), across(c0t)
    (state_b1, state_c0), (part_b1, part_c0) = forward(b1, core(b1), c0, core(c0))
    ((keep_a1, send_a1),), done = backward((state_a1,), part_a1, ya1)

    yb0, part_b1, send_a1 = meet(yb0, part_b1, send_a1)
    yb1 = exchange(part_b1)
    ka1 = core(send_a1)
    qc1 = core(c1c), core(c1t)
    ((keep_b0, send_b0),), done = backward((state_b0,), part_b0, yb0)
    kb0 = core(send_b0)

    part_c0, ka1, yb1, kb0, *qc1 = meet(part_c0, ka1, yb1, kb0, *qc1)
    yc0 = exchange(part_c0)
    ra = across(add(keep_a1, ka1))
    sum1 = add(keep1, k1)
    sumb0 = add(keep_b0, kb0)
    ((keep_b1, send_b1),), done = backward((state_b1,), part_b1, yb1)
    kb1 = core(send_b1)
    (state_c1,), (part_c1,) = forward((c1c, c1t), tuple(qc1))

    suma = add(keep_a0, ka0, ra)
    part_c1, yc0, suma, sum1, sumb0, keep_b1 = meet(part_c1, yc0, suma, sum1, sumb0, keep_b1)
    yc1 = exchange(part_c1)
    rb = across(add(keep_b1, kb1))
    from_a = outer_z(suma)
    ((keep_c0, send_c0),), done = backward((state_c0,), part_c0, yc0)
    kc0 = core(send_c0)

    yc1, rb, from_a, part0, keep_c0 = meet(yc1, rb, from_a, part0, keep_c0)
    y0 = exchange(part0)
    ((keep_c1, send_c1),), done = backward((state_c1,), part_c1, yc1)
    kc1 = core(send_c1)
    sumc0 = add(keep_c0, kc0)
    sumb = add(sumb0, rb)
    b_edge, b_middle = swap(sumb, 8, (0, 3)), swap(sumb, 12, (1, 2))

    sumc1 = add(keep_c1, kc1)
    rc = across(sumc1)
    rc, sum1 = meet(rc, sum1)
    sumc = add(sumc0, rc)
    c_edge = outer_z(sumc, part=(0, 3))
    r0 = across(sum1)
    y0, _ = meet(y0, sumc)
    ((keep0, send0),), done = backward((state0,), part0, y0)
    k0 = core(send0)

    inputs, scaled = zip(*rights)
    hidden, grad_gate, grad_up = zip(*lefts)
    gate_grad = outer(grad_gate, inputs)

    c_edge, b_edge, b_middle, _ = meet(c_edge, b_edge, b_middle, gate_grad)
    sumc = add(sumc, c_edge)
    sumc, k0 = meet(sumc, k0)
    far = swap(sumc, 8, (1, 2))
    grad_up, _ = meet(grad_up, sumc)
    up_grad = outer(grad_up, inputs)
    hidden, _ = meet(hidden, up_grad)
    down_grad = outer(hidden, scaled)
    r0, _ = meet(r0, down_grad)
    near = add(keep0, k0, r0, from_a, b_edge, b_middle)
    far, near = meet(far, near)
    token_grads, by_expert = finish(near, far)
    chosen = expert_ids[:, :, None] == jnp.arange(experts, dtype=jnp.int32)[None, None, :]
    prob_grads = jnp.sum(jnp.where(chosen, by_expert[:, None, :experts], 0.0), axis=2)
    return (
        token_grads,
        prob_grads,
        gate_grad[None],
        up_grad[None],
        down_grad[None],
    )


def solution(mesh):
    dense = mesh.shape["expert"] == 16 and mesh.shape["dp"] == 2
    return jax.shard_map(
        local_dense if dense else local_general,
        mesh=mesh,
        in_specs=(
            P("expert", "dp"),
            P("expert", "dp"),
            P("expert", None),
            P("expert", None),
            P("expert", None, "dp"),
            P("expert", None, "dp"),
            P("expert", None, "dp"),
        ),
        out_specs=(
            P("expert", "dp"),
            P("expert", None),
            P("expert", None, "dp"),
            P("expert", None, "dp"),
            P("expert", None, "dp"),
        ),
        check_vma=False,
    )
```

```python
import functools

import jax
import jax.numpy as jnp
from jax import lax
from jax.experimental import pallas as pl
from jax.experimental.pallas import tpu as pltpu
from jax.sharding import PartitionSpec as P

F32 = jnp.float32
BF16 = jnp.bfloat16
LANES = 128
VMEM = 14 * 1024 * 1024


def contract_last(left_matrix, right_matrix):
    return lax.dot_general(
        left_matrix, right_matrix, (((1,), (1,)), ((), ())), preferred_element_type=jnp.float32
    )


def contract_first(left_matrix, right_matrix):
    return lax.dot_general(
        left_matrix, right_matrix, (((0,), (0,)), ((), ())), preferred_element_type=jnp.float32
    )


def activations(gate_value, up_value, back_value, weights):
    sigmoid_gate = jax.nn.sigmoid(gate_value)
    silu_gate = gate_value * sigmoid_gate
    hidden = (silu_gate * up_value).astype(jnp.bfloat16)
    prob_local = jnp.sum(hidden.astype(jnp.float32) * back_value, axis=1, keepdims=True)
    grad_back = weights * back_value
    grad_gate = (
        grad_back * up_value * sigmoid_gate * (1.0 + gate_value * (1.0 - sigmoid_gate))
    ).astype(jnp.bfloat16)
    grad_up = (grad_back * silu_gate).astype(jnp.bfloat16)
    return (hidden, grad_gate, grad_up, prob_local)


def local_general(tokens, cotangent, router_probs, expert_ids, w_gate, w_up, w_down):
    experts = lax.axis_size("expert")
    local_tokens, top_count = expert_ids.shape
    row_count = local_tokens * top_count
    slot_count = min(local_tokens, max(2, (row_count + experts - 1) // experts * 17 // 16))
    features = tokens.shape[1]
    flat_ids = expert_ids.reshape(-1)
    hit_table = (flat_ids[:, None] == jnp.arange(experts, dtype=jnp.int32)[None, :]).astype(
        jnp.int32
    )
    slot_ranks = jnp.sum(jnp.cumsum(hit_table, axis=0) * hit_table, axis=1) - 1
    slot_places = flat_ids * slot_count + slot_ranks
    slot_table = jnp.full((experts * slot_count,), row_count, jnp.int32)
    slot_table = slot_table.at[slot_places].set(jnp.arange(row_count, dtype=jnp.int32))
    filled = slot_table < row_count
    sources = jnp.minimum(slot_table, row_count - 1)
    owners = sources // top_count
    send_probs = jnp.where(
        filled, router_probs.reshape(-1)[sources], jnp.zeros((), router_probs.dtype)
    )
    send_probs = send_probs.reshape(experts, slot_count)

    def pack_rows(source):
        picked = jnp.where(filled[:, None], source[owners], jnp.zeros((), source.dtype))
        return picked.reshape(experts, slot_count, source.shape[1])

    exchange = functools.partial(
        lax.all_to_all, axis_name="expert", split_axis=0, concat_axis=0, tiled=True
    )
    recv_in, recv_grad, recv_probs = (
        exchange(pack_rows(tokens)),
        exchange(pack_rows(cotangent)),
        exchange(send_probs),
    )
    inputs = recv_in.reshape(experts * slot_count, features)
    grads_in = recv_grad.reshape(experts * slot_count, features)
    weights = recv_probs.reshape(-1).astype(jnp.float32)
    weight_gate = w_gate[0]
    weight_up = w_up[0]
    weight_down = w_down[0]
    gate_part = contract_last(inputs, weight_gate)
    up_part = contract_last(inputs, weight_up)
    back_part = contract_last(grads_in, weight_down)
    gate_value, up_value, back_value = (
        lax.psum(gate_part.astype(jnp.bfloat16), "dp").astype(jnp.float32),
        lax.psum(up_part.astype(jnp.bfloat16), "dp").astype(jnp.float32),
        lax.psum(back_part.astype(jnp.bfloat16), "dp").astype(jnp.float32),
    )
    hidden, grad_gate, grad_up, prob_value = activations(
        gate_value, up_value, back_value, weights[:, None]
    )
    scaled = (weights[:, None] * grads_in).astype(jnp.bfloat16)
    row_term = jnp.dot(grad_gate, weight_gate, preferred_element_type=jnp.float32)
    row_term = (row_term + jnp.dot(grad_up, weight_up, preferred_element_type=jnp.float32)).astype(
        jnp.bfloat16
    )
    gate_grad = contract_first(grad_gate, inputs).astype(jnp.bfloat16)
    up_grad = contract_first(grad_up, inputs).astype(jnp.bfloat16)
    down_grad = contract_first(hidden, scaled).astype(jnp.bfloat16)
    back_terms = exchange(row_term.reshape(experts, slot_count, features))
    back_probs = exchange(prob_value.astype(jnp.bfloat16).reshape(experts, slot_count))
    returned = back_terms.reshape(experts * slot_count, features)[slot_places].astype(jnp.float32)
    token_sum = jnp.sum(returned.reshape(local_tokens, top_count, features), axis=1)
    prob_grads = (
        back_probs.reshape(-1)[slot_places].astype(jnp.float32).reshape(local_tokens, top_count)
    )
    return (
        token_sum.astype(jnp.bfloat16),
        prob_grads,
        gate_grad[None],
        up_grad[None],
        down_grad[None],
    )


def kernel_call(body, operands, outs, scratch=(), name=None):
    return pl.pallas_call(
        body,
        in_specs=[pl.BlockSpec(memory_space=pltpu.VMEM)] * len(operands),
        out_specs=[pl.BlockSpec(memory_space=pltpu.VMEM)] * len(outs),
        out_shape=[jax.ShapeDtypeStruct(shape, dtype) for shape, dtype in outs],
        scratch_shapes=list(scratch),
        compiler_params=pltpu.CompilerParams(vmem_limit_bytes=VMEM),
        cost_estimate=pl.CostEstimate(flops=1000, bytes_accessed=1000, transcendentals=0),
        name=name,
    )(*operands)


def choose_kernel(cuts, first, second, *outs):
    z_index = lax.div(lax.axis_index("expert"), 4)
    edge = (z_index == 0) | (z_index == 3)

    def write(source):
        for (start, end), out in zip(cuts, outs):
            out[...] = source[:, start:end]

    @pl.when(edge)
    def _():
        write(first)

    @pl.when(jnp.logical_not(edge))
    def _():
        write(second)


def choose(first, second, *cuts):
    return kernel_call(
        functools.partial(choose_kernel, cuts),
        (first, second),
        [((first.shape[0], end - start), BF16) for start, end in cuts],
        name="choose",
    )


def tiles(width, tile, body):
    @pl.loop(0, width // tile)
    def _(k):
        body(pl.multiple_of(k * tile, tile))


def pack_kernel(tokens, cotangent, probs, ids, out, ids_here, packed, sems):
    rows, width = tokens.shape
    moves = (
        (ids, ids_here),
        (cotangent, packed.at[:, pl.ds(0, width)]),
        (tokens, packed.at[:, pl.ds(width, width)]),
        (packed, out),
    )
    copies = [
        pltpu.make_async_copy(source, target, sems.at[i])
        for i, (source, target) in enumerate(moves)
    ]
    for copy in copies[:3]:
        copy.start()
    copies[0].wait()
    lane = lax.broadcasted_iota(jnp.int32, (rows, LANES), 1)
    routing = jnp.full((rows, LANES), -1.0, F32)
    weights, choices = probs[...].astype(F32).T, ids_here[...].T
    for k in range(choices.shape[1]):
        routing = jnp.where(lane == choices[:, k : k + 1], weights[:, k : k + 1], routing)
    packed[:, pl.ds(2 * width, LANES)] = routing.astype(BF16)
    copies[1].wait()
    copies[2].wait()
    copies[3].start()
    copies[3].wait()


def pack(tokens, cotangent, probs, ids):
    rows, width = tokens.shape
    columns = 2 * width + LANES
    return pl.pallas_call(
        pack_kernel,
        in_specs=[pl.BlockSpec(memory_space=pl.ANY)] * 2
        + [pl.BlockSpec(memory_space=pltpu.VMEM), pl.BlockSpec(memory_space=pl.ANY)],
        out_specs=pl.BlockSpec(memory_space=pl.ANY),
        out_shape=jax.ShapeDtypeStruct((rows, columns), BF16),
        scratch_shapes=[
            pltpu.VMEM(ids.shape, ids.dtype),
            pltpu.VMEM((rows, columns), BF16),
            pltpu.SemaphoreType.DMA((4,)),
        ],
        compiler_params=pltpu.CompilerParams(vmem_limit_bytes=60 * 1024 * 1024),
        cost_estimate=pl.CostEstimate(flops=1000, bytes_accessed=1000, transcendentals=0),
        name="pack",
    )(tokens, cotangent, probs, ids)


def front_kernel(slots, layout, joined, *refs):
    sources = refs[: sum(layout)]
    w_gate, w_up, w_down = refs[len(sources) : len(sources) + 3]
    *outs, acc, picks = refs[len(sources) + 3 :]
    units, width = w_gate.shape
    block = sources[0].shape[0]
    pairs = len(layout) // 2
    rows = picks.shape[1]
    tile = 1024
    expert = lax.axis_index("expert")

    blocks, start = [], 0
    for size in layout:
        here = sources[start : start + size]
        blocks.append((here[0], here[-1], width if size == 1 else 0))
        start = start + size

    lane = lax.broadcasted_iota(jnp.int32, (block, LANES), 1)
    tri = (
        lax.broadcasted_iota(jnp.int32, (block, block), 1)
        <= lax.broadcasted_iota(jnp.int32, (block, block), 0)
    ).astype(BF16)
    for p in range(pairs):
        spread, weights = outs[4 * p + 2], outs[4 * p + 3]
        total = jnp.zeros((rows, LANES), F32)
        for b, (_, source, offset) in enumerate(blocks[2 * p : 2 * p + 2]):
            routing = source[:, pl.ds(offset + width, LANES)].astype(F32)
            prob = jnp.sum(jnp.where(lane == expert, routing, 0.0), axis=1, keepdims=True)
            chosen = jnp.broadcast_to(prob >= 0.0, (block, LANES))
            rank = jnp.dot(tri, chosen.astype(BF16), preferred_element_type=F32)
            slot = jnp.where(chosen, rank + (slots * b - 1.0), -1.0)
            spread[pl.ds(b * block, block), :] = (
                lax.broadcasted_iota(jnp.int32, (block, rows), 1)
                == slot[:, :1].astype(jnp.int32)
            ).astype(BF16)
            slot_row = slot.T[:1, :].astype(jnp.int32)
            picked = (lax.broadcasted_iota(jnp.int32, (rows, block), 0) == slot_row).astype(BF16)
            picks[p, :, pl.ds(b * block, block)] = picked
            prob = jnp.broadcast_to(jnp.maximum(prob, 0.0), (block, LANES)).astype(BF16)
            total = total + jnp.dot(picked, prob, preferred_element_type=F32)
        weights[...] = total
    acc[...] = jnp.zeros(acc.shape, F32)

    def step(start):
        here = pl.ds(start, tile)
        rows_in, grads_in = [], []
        for p in range(pairs):
            inputs, scaled, _, weights = outs[4 * p : 4 * p + 4]
            (first_c, first_t, first_at), (second_c, second_t, second_at) = blocks[2 * p : 2 * p + 2]
            stacked = jnp.concatenate(
                [
                    first_t[:, pl.ds(first_at + start, tile)],
                    second_t[:, pl.ds(second_at + start, tile)],
                ],
                axis=0,
            )
            picked = jnp.dot(picks[p], stacked, preferred_element_type=F32).astype(BF16)
            inputs[:, here] = picked
            rows_in.append(picked)
            stacked = jnp.concatenate([first_c[:, here], second_c[:, here]], axis=0)
            picked = jnp.dot(picks[p], stacked, preferred_element_type=F32)
            scaled[:, here] = (weights[:, :1] * picked).astype(BF16)
            grads_in.append(picked.astype(BF16))
        rows_in = jnp.concatenate(rows_in, axis=0)
        acc[:, :units] += contract_last(rows_in, w_gate[:, here])
        acc[:, units : 2 * units] += contract_last(rows_in, w_up[:, here])
        acc[:, 2 * units :] += contract_last(jnp.concatenate(grads_in, axis=0), w_down[:, here])

    tiles(width, tile, step)
    if joined:
        outs[-1][...] = jnp.concatenate(
            [acc[p * rows : p * rows + 2 * slots] for p in range(pairs)], axis=0
        ).astype(BF16)
    else:
        for p in range(pairs):
            outs[4 * pairs + p][...] = acc[p * rows : p * rows + 2 * slots].astype(BF16)


def front(blocks, w_gate, w_up, w_down, slots, joined):
    blocks = [b if isinstance(b, tuple) else (b,) for b in blocks]
    layout = [len(b) for b in blocks]
    sources = [array for b in blocks for array in b]
    block = sources[0].shape[0]
    units, width = w_gate.shape
    pairs = len(blocks) // 2
    rows = -(-2 * slots // 16) * 16
    results = kernel_call(
        functools.partial(front_kernel, slots, layout, joined),
        (*sources, w_gate, w_up, w_down),
        [
            ((rows, width), BF16),
            ((rows, width), BF16),
            ((2 * block, rows), BF16),
            ((rows, LANES), F32),
        ]
        * pairs
        + [((2 * slots * (pairs if joined else 1), 3 * units), BF16)] * (1 if joined else pairs),
        scratch=[
            pltpu.VMEM((pairs * rows, 3 * units), F32),
            pltpu.VMEM((pairs, rows, 2 * block), BF16),
        ],
        name="front",
    )
    names = ("inputs", "scaled", "spread", "weights")
    states = [dict(zip(names, results[4 * p : 4 * p + 4])) for p in range(pairs)]
    return states, results[4 * pairs :]


def back_kernel(pairs, own, peer, *refs):
    weights, spreads = refs[:pairs], refs[pairs : 2 * pairs]
    w_gate, w_up, hidden, grad_gate, grad_up, *outs = refs[2 * pairs :]
    units, width = w_gate.shape
    filled = own.shape[0] // pairs
    tokens, rows = spreads[0].shape
    tile = 1024
    expert = lax.axis_index("expert")

    def place(term, columns):
        for p in range(pairs):
            here = term[p * rows : (p + 1) * rows]
            placed = jnp.dot(spreads[p][...], here, preferred_element_type=F32).astype(BF16)
            outs[2 * p][:, columns] = placed[: tokens // 2]
            outs[2 * p + 1][:, columns] = placed[tokens // 2 :]

    def value(i):
        columns = pl.ds(i * units, units)
        total = own[:, columns].astype(F32) + peer[:, columns].astype(F32)
        if rows == filled:
            return total
        pad = jnp.zeros((rows - filled, units), F32)
        pieces = [total[p * filled : (p + 1) * filled] for p in range(pairs)]
        return jnp.concatenate([piece for each in pieces for piece in (each, pad)], axis=0)

    scales = jnp.concatenate([weight[:, :1] for weight in weights], axis=0)
    h, gg, gu, prob = activations(value(0), value(1), value(2), scales)
    hidden[...] = h
    grad_gate[...] = gg
    grad_up[...] = gu
    lane = lax.broadcasted_iota(jnp.int32, (pairs * rows, LANES), 1)
    place(jnp.where(lane == expert, prob, 0.0).astype(BF16), pl.ds(width, LANES))

    def step(start):
        columns = pl.ds(start, tile)
        term = jnp.dot(grad_gate[...], w_gate[:, columns], preferred_element_type=F32)
        term = term + jnp.dot(grad_up[...], w_up[:, columns], preferred_element_type=F32)
        place(term.astype(BF16), columns)

    tiles(width, tile, step)


def back(states, own, peer, w_gate, w_up):
    units, width = w_gate.shape
    pairs = len(states)
    tokens, rows = states[0]["spread"].shape
    half = (tokens // 2, width + LANES)
    results = kernel_call(
        functools.partial(back_kernel, pairs),
        (
            own,
            peer,
            *[state["weights"] for state in states],
            *[state["spread"] for state in states],
            w_gate,
            w_up,
        ),
        [((pairs * rows, units), BF16)] * 3 + [(half, BF16)] * (2 * pairs),
        name="back",
    )
    return results[:3], [results[3 + 2 * p : 5 + 2 * p] for p in range(pairs)]


def outer_kernel(count, *refs):
    *terms, out, turned = refs
    lefts, rights = terms[:count], terms[count:]

    @pl.when(pl.program_id(0) == 0)
    def _():
        turned[...] = jnp.concatenate([left[...] for left in lefts], axis=0).T

    right = jnp.concatenate([right[...] for right in rights], axis=0)
    out[...] = jnp.dot(turned[...], right, preferred_element_type=F32).astype(BF16)


def outer(lefts, rights):
    units, width = lefts[0].shape[1], rights[0].shape[1]
    rows = sum(left.shape[0] for left in lefts)
    tile = 1024
    return pl.pallas_call(
        functools.partial(outer_kernel, len(lefts)),
        grid=(width // tile,),
        in_specs=[pl.BlockSpec(left.shape, lambda k: (0, 0)) for left in lefts]
        + [pl.BlockSpec((right.shape[0], tile), lambda k: (0, k)) for right in rights],
        out_specs=pl.BlockSpec((units, tile), lambda k: (0, k)),
        out_shape=jax.ShapeDtypeStruct((units, width), BF16),
        scratch_shapes=[pltpu.VMEM((units, rows), BF16)],
        compiler_params=pltpu.CompilerParams(vmem_limit_bytes=VMEM),
        cost_estimate=pl.CostEstimate(flops=1000, bytes_accessed=1000, transcendentals=0),
        name="outer",
    )(*lefts, *rights)


def add_kernel(*refs):
    *terms, out = refs
    total = terms[0][...].astype(F32)
    for term in terms[1:]:
        total = total + term[...].astype(F32)
    out[...] = total.astype(BF16)


def add(*terms):
    return kernel_call(add_kernel, terms, [(terms[0].shape, BF16)], name="add")[0]


def finish_kernel(*refs):
    *terms, tokens_out, probs_out = refs
    total = terms[0][...].astype(F32)
    for term in terms[1:]:
        total = total + term[...].astype(F32)
    width = tokens_out.shape[1]
    tokens_out[...] = total[:, :width].astype(BF16)
    probs_out[...] = total[:, width:]


def finish(*terms):
    block, columns = terms[0].shape
    outs = [((block, columns - LANES), BF16), ((block, LANES), F32)]
    return kernel_call(finish_kernel, terms, outs, name="finish")


def meet(*values):
    return lax.optimization_barrier(values)


def local_dense(tokens, cotangent, router_probs, expert_ids, w_gate, w_up, w_down):
    experts = lax.axis_size("expert")
    block, top_count = expert_ids.shape
    row_count = block * top_count
    slots = min(block, max(2, (row_count + experts - 1) // experts * 17 // 16))
    weight_gate, weight_up, weight_down = w_gate[0], w_up[0], w_down[0]

    def swap(value, bits, part=(0, 1, 2, 3)):
        pairs = [(i, i ^ bits) for i in range(experts) if i // 4 in part]
        return lax.ppermute(value, "expert", pairs)

    core = functools.partial(swap, bits=1)
    across = functools.partial(swap, bits=2)
    outer_z = functools.partial(swap, bits=4)
    inner_z = functools.partial(swap, bits=12, part=(1, 2))

    rights, lefts = [], []

    def forward(*blocks, joined=False):
        return front(blocks, weight_gate, weight_up, weight_down, slots, joined)

    def exchange(part):
        return lax.ppermute(part, "dp", [(0, 1), (1, 0)])

    def backward(states, own, peer):
        left, sums = back(states, own, peer, weight_gate, weight_up)
        rights.extend((state["inputs"], state["scaled"]) for state in states)
        lefts.append(left)
        return sums, left[0]

    features = tokens.shape[1]
    all_columns = 2 * features + LANES

    p0 = pack(tokens, cotangent, router_probs.T, expert_ids.T)
    q0 = core(p0)
    p1, a0, m0 = across(p0), outer_z(p0), inner_z(p0)
    (state0,), (part0,) = forward(p0, q0)

    p1, a0, m0, part0 = meet(p1, a0, m0, part0)
    a1, b0e, c0m = across(a0), outer_z(m0), inner_z(a0)
    states1, (part1,) = forward(p1, core(p1), a0, core(a0), joined=True)
    y1 = exchange(part1)

    (b0,) = choose(b0e, m0, (0, all_columns))
    a1, b0, c0m, _ = meet(a1, b0, c0m, part1)
    b1, c0e = across(b0), outer_z(c0m)
    (state_a1, state_b0), (part_a1, part_b0) = forward(a1, core(a1), b0, core(b0))

    y1, part_a1 = meet(y1, part_a1)
    ya1 = exchange(part_a1)
    ((keep1, send1), (keep_a0, send_a0)), done = backward(states1, part1, y1)
    k1, ka0 = core(send1), core(send_a0)

    columns = (0, all_columns), (0, features), (features, all_columns)
    c0, c0c, c0t = choose(c0e, c0m, *columns)
    b1, c0, c0c, c0t, ya1, part_b0, k1, ka0 = meet(
        b1, c0, c0c, c0t, ya1, part_b0, k1, ka0
    )
    yb0 = exchange(part_b0)
    c1c, c1t = across(c0c), across(c0t)
    (state_b1, state_c0), (part_b1, part_c0) = forward(b1, core(b1), c0, core(c0))
    ((keep_a1, send_a1),), done = backward((state_a1,), part_a1, ya1)

    yb0, part_b1, send_a1 = meet(yb0, part_b1, send_a1)
    yb1 = exchange(part_b1)
    ka1 = core(send_a1)
    qc1 = core(c1c), core(c1t)
    ((keep_b0, send_b0),), done = backward((state_b0,), part_b0, yb0)
    kb0 = core(send_b0)

    part_c0, ka1, yb1, kb0, *qc1 = meet(part_c0, ka1, yb1, kb0, *qc1)
    yc0 = exchange(part_c0)
    ra = across(add(keep_a1, ka1))
    sum1 = add(keep1, k1)
    sumb0 = add(keep_b0, kb0)
    ((keep_b1, send_b1),), done = backward((state_b1,), part_b1, yb1)
    kb1 = core(send_b1)
    (state_c1,), (part_c1,) = forward((c1c, c1t), tuple(qc1))

    suma = add(keep_a0, ka0, ra)
    part_c1, yc0, suma, sum1, sumb0, keep_b1 = meet(part_c1, yc0, suma, sum1, sumb0, keep_b1)
    yc1 = exchange(part_c1)
    rb = across(add(keep_b1, kb1))
    from_a = outer_z(suma)
    ((keep_c0, send_c0),), done = backward((state_c0,), part_c0, yc0)
    kc0 = core(send_c0)

    yc1, rb, from_a, part0, keep_c0 = meet(yc1, rb, from_a, part0, keep_c0)
    y0 = exchange(part0)
    ((keep_c1, send_c1),), done = backward((state_c1,), part_c1, yc1)
    kc1 = core(send_c1)
    sumc0 = add(keep_c0, kc0)
    sumb = add(sumb0, rb)
    b_edge, b_middle = swap(sumb, 8, (0, 3)), swap(sumb, 12, (1, 2))

    sumc1 = add(keep_c1, kc1)
    rc = across(sumc1)
    rc, sum1 = meet(rc, sum1)
    sumc = add(sumc0, rc)
    c_edge = outer_z(sumc)
    r0 = across(sum1)
    y0, _ = meet(y0, sumc)
    ((keep0, send0),), done = backward((state0,), part0, y0)
    k0 = core(send0)

    inputs, scaled = zip(*rights)
    hidden, grad_gate, grad_up = zip(*lefts)
    gate_grad = outer(grad_gate, inputs)

    c_edge, b_edge, b_middle, _ = meet(c_edge, b_edge, b_middle, gate_grad)
    sumc = add(sumc, c_edge)
    sumc, k0 = meet(sumc, k0)
    far = swap(sumc, 8, (1, 2))
    grad_up, _ = meet(grad_up, sumc)
    up_grad = outer(grad_up, inputs)
    hidden, _ = meet(hidden, up_grad)
    down_grad = outer(hidden, scaled)
    r0, _ = meet(r0, down_grad)
    near = add(keep0, k0, r0, from_a, b_edge, b_middle)
    far, near = meet(far, near)
    token_grads, by_expert = finish(near, far)
    chosen = expert_ids[:, :, None] == jnp.arange(experts, dtype=jnp.int32)[None, None, :]
    prob_grads = jnp.sum(jnp.where(chosen, by_expert[:, None, :experts], 0.0), axis=2)
    return (
        token_grads,
        prob_grads,
        gate_grad[None],
        up_grad[None],
        down_grad[None],
    )


def solution(mesh):
    dense = mesh.shape["expert"] == 16 and mesh.shape["dp"] == 2
    return jax.shard_map(
        local_dense if dense else local_general,
        mesh=mesh,
        in_specs=(
            P("expert", "dp"),
            P("expert", "dp"),
            P("expert", None),
            P("expert", None),
            P("expert", None, "dp"),
            P("expert", None, "dp"),
            P("expert", None, "dp"),
        ),
        out_specs=(
            P("expert", "dp"),
            P("expert", None),
            P("expert", None, "dp"),
            P("expert", None, "dp"),
            P("expert", None, "dp"),
        ),
        check_vma=False,
    )
```
